32 devices in a mesh: grp: 1, kz: 32 (over z, y, x, core).
Axes of the slice: x: 2, y: 2, z: 4, core: 2. Of those that a mesh axis runs over, the one named last changes fastest.
Arguments:
- kspace: float32 [8, 16, 512, 512], P('grp', None, 'kz'), may hold values from -8 to 8
- sensitivity: float32 [2, 256, 8, 16, 512], P(None, ('grp', 'kz')), may hold values from -2 to 2
- weight_first: bfloat16 [24, 2, 3, 3, 3], replicated, may hold values from -0.875 to 0.875
- bias_first: float32 [24], replicated, may hold values from -0.5 to 0.5
- weight_second: bfloat16 [24, 24, 3, 3, 3], replicated, may hold values from -0.3125 to 0.3125
- bias_second: float32 [24], replicated, may hold values from -0.5 to 0.5
- weight_third: bfloat16 [24, 24, 3, 3, 3], replicated, may hold values from -0.3125 to 0.3125
- bias_third: float32 [24], replicated, may hold values from -0.5 to 0.5
Outputs:
- features: bfloat16 [24, 512, 16, 256], P('grp', 'kz')
The draws below stay inside these ranges and needn't reach their ends.
All inputs are finite; a program needn't handle non-finite values.
Results may differ from the reference program's by a relative error of at most 0.0058.
Values may be sent and summed in bfloat16 or wider, within the bound.
No kernel may reach another device: no remote copies, remote signals or barrier semaphores. Data moves between devices by JAX's collectives and lax.ppermute only.
A program may use at most 192 MiB of HBM per device.

```python
import math
import jax
import jax.numpy as jnp
from jax import lax

COILS = 8
KY = 256
KZ = 512
X = 16
CIN = 2
CH = 24


def level_of(key, dims, split, smallest, high):
    factor_of = 1.0
    for axis_at, shards_of in split:
        steps = jax.random.uniform(jax.random.fold_in(jax.random.fold_in(key, 6), axis_at), (shards_of,), jnp.float32, smallest / len(split), high / len(split))
        factor_of = factor_of * jnp.repeat(jnp.exp(steps), dims[axis_at] // shards_of).reshape((-1,) + (1,) * (len(dims) - 1 - axis_at))
    return factor_of


def centred(own_key, extent, spread, limit, shards=(), kind=jnp.bfloat16):
    drawn = jax.random.normal(own_key, extent, jnp.float32) * spread
    if len(shards) > 0:
        drawn = level_of(own_key, extent, shards, -0.22, 0.18) * drawn
    return jnp.clip(drawn, min=-limit, max=limit).astype(kind)


def setup_inputs(seed: int = 0, part: int = 0) -> dict:
    seeds = jax.random.split(jax.random.key(seed), 9)
    part_splits = jax.random.split(jax.random.fold_in(seeds[8], part), 9)
    kspace = centred(part_splits[0], (COILS, X, KZ, 2 * KY), 1.0, 8.0, ((2, 32),), jnp.float32)
    sensitivity = centred(part_splits[1], (2, KY, COILS, X, KZ), 0.25, 2.0, ((1, 32),), jnp.float32)
    weight_first = centred(seeds[2], (CH, CIN, 3, 3, 3), (27 * CIN) ** -0.5, 0.875)
    bias_first = jnp.clip(jax.random.uniform(seeds[3], (CH,), jnp.float32, -0.5, 0.5), -0.5, 0.5)
    weight_second = centred(seeds[4], (CH, CH, 3, 3, 3), (27 * CH // 2) ** -0.5, 0.3125)
    bias_second = jnp.clip(jax.random.uniform(seeds[5], (CH,), jnp.float32, -0.5, 0.5), -0.5, 0.5)
    weight_third = centred(seeds[6], (CH, CH, 3, 3, 3), (27 * CH // 2) ** -0.5, 0.3125)
    bias_third = jnp.clip(jax.random.uniform(seeds[7], (CH,), jnp.float32, -0.5, 0.5), -0.5, 0.5)
    return {"kspace": kspace, "sensitivity": sensitivity, "weight_first": weight_first, "bias_first": bias_first, "weight_second": weight_second, "bias_second": bias_second, "weight_third": weight_third, "bias_third": bias_third}


HIGHEST_PRECISION = lax.Precision.HIGHEST

def dft_parts(length):
    positions = jnp.arange(length, dtype=jnp.int32)
    phase_int = positions[:, None] * positions[None, :] % length
    angles = phase_int.astype(jnp.float32) * (2.0 * math.pi / length)
    factor = 1.0 / math.sqrt(length)
    return (jnp.cos(angles) * factor, jnp.sin(angles) * factor)

def y_table(length):
    cosine, sine_part = dft_parts(length)
    upper = jnp.concatenate([cosine, sine_part], axis=1)
    lower = jnp.concatenate([-sine_part, cosine], axis=1)
    return jnp.concatenate([upper, lower], axis=0)

def z_table(length):
    cosine, sine_part = dft_parts(length)
    return jnp.stack([jnp.stack([cosine, sine_part], axis=1), jnp.stack([-sine_part, cosine], axis=1)], axis=0)

def combine(sensitivity, coil_images):
    sens_re = sensitivity[0]
    sens_im = sensitivity[1]
    coil_re = coil_images[0]
    coil_im = coil_images[1]
    merged_re = lax.optimization_barrier(jnp.sum(sens_re * coil_re + sens_im * coil_im, axis=1))
    merged_im = lax.optimization_barrier(jnp.sum(sens_re * coil_im - sens_im * coil_re, axis=1))
    return jnp.stack([merged_re, merged_im], axis=0).astype(jnp.bfloat16)

def convolve_exact(volume, weight, bias_vec):
    widened = lax.optimization_barrier(volume).astype(jnp.float32)
    result = lax.conv_general_dilated(widened[None], weight.astype(jnp.float32), (1, 1, 1), [(1, 1), (1, 1), (1, 1)], dimension_numbers=('NCDHW', 'OIDHW', 'NCDHW'), precision=HIGHEST_PRECISION)[0]
    return jnp.maximum(result + bias_vec[:, None, None, None], 0.0).astype(jnp.bfloat16)

def reference(kspace, sensitivity, weight_first, bias_first, weight_second, bias_second, weight_third, bias_third):
    y_lines = jnp.dot(kspace.reshape(-1, 2 * KY), y_table(KY), precision=HIGHEST_PRECISION, preferred_element_type=jnp.float32)
    y_lines = y_lines.reshape(COILS, X, KZ, 2, KY)
    coil_images = jnp.einsum('cxkry,rkpz->pycxz', y_lines, z_table(KZ), precision=HIGHEST_PRECISION)
    activity = jnp.transpose(combine(sensitivity, coil_images), (0, 3, 2, 1))
    for weight, bias_vec in ((weight_first, bias_first), (weight_second, bias_second), (weight_third, bias_third)):
        activity = convolve_exact(activity, weight, bias_vec)
    return activity
```

```python
import functools
import math

import jax
import jax.numpy as jnp
import numpy as np
from jax import lax
from jax.experimental import pallas as pl
from jax.experimental.pallas import tpu as pltpu
from jax.sharding import PartitionSpec as P

BF16 = jnp.bfloat16
F32 = jnp.float32
HALO = 3
WINDOW = 256
VMEM_LIMIT = 56 * 1024 * 1024


def round_up(value, unit):
    return -(-value // unit) * unit


def params():
    return pltpu.CompilerParams(vmem_limit_bytes=VMEM_LIMIT)


def vmem_spec():
    return pl.BlockSpec(memory_space=pltpu.VMEM)


def halves(table):
    high = table.astype(jnp.bfloat16)
    low = (table - high.astype(np.float64)).astype(jnp.bfloat16)
    return high, low


def trig(length, rows, cols):
    phase = (rows[:, None] * cols[None, :]) % length
    angle = phase * (2.0 * math.pi / length)
    return np.cos(angle), np.sin(angle)


def y_table(y_count, devices):
    y_here = y_count // devices
    order = (np.arange(devices)[None, :] * y_here + np.arange(y_here)[:, None]).reshape(-1)
    cosine, sine = trig(y_count, order, np.arange(y_count))
    real = np.concatenate([cosine, -sine], axis=1)
    imag = np.concatenate([sine, cosine], axis=1)
    table = np.stack([real, imag], axis=1).reshape(2 * y_count, 2 * y_count)
    return table / math.sqrt(y_count)


def z_table(z_count, devices):
    cosine, sine = trig(z_count, np.arange(z_count), np.arange(z_count))
    real = np.concatenate([cosine, sine], axis=1)
    imag = np.concatenate([-sine, cosine], axis=1)
    table = np.stack([real, imag], axis=0).reshape(2, devices, z_count // devices, 2 * z_count)
    return np.transpose(table, (1, 0, 2, 3)).reshape(2 * z_count, 2 * z_count)


def y_kernel(devices, k_ref, t_ref, out_ref, lines, turned, sems):
    pairs, kz_here, width = lines.shape[1], lines.shape[0], lines.shape[2]
    rows = t_ref.shape[0]

    def fetch(kz):
        return pltpu.make_async_copy(k_ref.at[:, kz, :], lines.at[kz], sems.at[kz])

    for kz in range(kz_here):
        fetch(kz).start()
    for kz in range(kz_here):
        fetch(kz).wait()
        line = lines[kz]
        high = line.astype(BF16)
        low = (line - high.astype(F32)).astype(BF16)
        operand = jnp.concatenate([high, high, low], axis=1)
        result = lax.dot_general(
            t_ref[...], operand, (((1,), (1,)), ((), ())), preferred_element_type=F32
        )
        turned[pl.ds(kz, rows, stride=kz_here), :] = result
    block = 2 * kz_here
    for row in range(rows // 2):
        y, device = row // devices, row % devices
        out_ref[device, :, y * pairs : (y + 1) * pairs] = turned[
            row * block : (row + 1) * block, :
        ].astype(BF16)


def y_transform(kspace, devices):
    coils, xs, kz_here, width = kspace.shape
    pairs = coils * xs
    y_count = width // 2
    high, low = halves(y_table(y_count, devices))
    table = jnp.asarray(np.concatenate([high, low, high], axis=1))
    return pl.pallas_call(
        functools.partial(y_kernel, devices),
        out_shape=jax.ShapeDtypeStruct((devices, 2 * kz_here, y_count // devices * pairs), BF16),
        in_specs=[pl.BlockSpec(memory_space=pl.ANY), vmem_spec()],
        out_specs=vmem_spec(),
        scratch_shapes=[
            pltpu.VMEM((kz_here, pairs, width), F32),
            pltpu.VMEM((2 * y_count * kz_here, pairs), F32),
            pltpu.SemaphoreType.DMA((kz_here,)),
        ],
        compiler_params=params(),
    )(kspace.reshape(pairs, kz_here, width), table)


def z_kernel(scale, devices, y_here, r_ref, t_ref, s_ref, out_ref, merged, turned):
    step = pl.program_id(0)
    coils, xs, z_count = s_ref.shape[2:]
    z_here = z_count // devices
    lines = r_ref[...].T
    operand = jnp.concatenate([lines, lines], axis=1)
    images = jnp.dot(operand, t_ref[...], preferred_element_type=F32)
    image_re = images[:, :z_count].reshape(coils, xs, z_count)
    image_im = images[:, z_count:].reshape(coils, xs, z_count)
    sens_re = s_ref[0, 0]
    sens_im = s_ref[1, 0]
    real = jnp.sum(sens_re * image_re + sens_im * image_im, axis=0) * scale
    imag = jnp.sum(sens_re * image_im - sens_im * image_re, axis=0) * scale
    base = pl.multiple_of(step * 2 * xs, 2 * xs)

    if merged.shape[0] > y_here * 2 * xs:

        @pl.when(step == 0)
        def _():
            merged[...] = jnp.zeros_like(merged)

    merged[pl.ds(base, 2 * xs), :] = jnp.concatenate([real, imag], axis=0)

    @pl.when(step == pl.num_programs(0) - 1)
    def _():
        lanes = merged.shape[0]
        rows = out_ref.shape[1]
        turned[...] = jnp.zeros_like(turned)
        turned[8 : 8 + z_count, :] = merged[...].T
        for device in range(devices):
            first = 8 + device * z_here - HALO
            out_ref[device] = turned[first : first + rows, :].astype(BF16)


def z_transform(received, sensitivity, devices):
    _, y_here, coils, xs, z_count = sensitivity.shape
    pairs = coils * xs
    high, low = halves(z_table(z_count, devices))
    table = jnp.asarray(np.concatenate([high, low], axis=0))
    scale = 1.0 / math.sqrt(z_count)
    rows = round_up(z_count // devices + 2 * HALO, 8)
    lanes = round_up(y_here * 2 * xs, 128)
    flat = received.reshape(2 * z_count, y_here * pairs)
    return pl.pallas_call(
        functools.partial(z_kernel, scale, devices, y_here),
        out_shape=jax.ShapeDtypeStruct((devices, rows, lanes), BF16),
        grid=(y_here,),
        in_specs=[
            pl.BlockSpec((2 * z_count, pairs), lambda y: (0, y)),
            pl.BlockSpec(table.shape, lambda y: (0, 0)),
            pl.BlockSpec((2, 1, coils, xs, z_count), lambda y: (0, y, 0, 0, 0)),
        ],
        out_specs=pl.BlockSpec((devices, rows, lanes), lambda y: (0, 0, 0)),
        scratch_shapes=[
            pltpu.VMEM((lanes, z_count), F32),
            pltpu.VMEM((8 + z_count + 32, lanes), F32),
        ],
        compiler_params=params(),
    )(flat, table, sensitivity)


def window_starts(lanes):
    return (0, lanes - WINDOW)


def column_map(xs, channels, x_major):
    half = xs // 2
    found = []
    for h in range(2):
        x, c = np.meshgrid(np.arange(half) + h * half, np.arange(channels), indexing="ij")
        if x_major:
            pad = np.full(WINDOW - half * channels, -9)
            x, c = x.reshape(-1), c.reshape(-1)
            order = [(pad, x), (pad, c)] if h else [(x, pad), (c, pad)]
            found.append((np.concatenate(order[0]), np.concatenate(order[1])))
        else:
            found.append((x.T.reshape(-1), c.T.reshape(-1)))
    return found


def band_masks(x_in, x_out):
    taps = np.arange(3)[:, None, None]
    return (x_in[None, :, None] == x_out[None, None, :] + taps - 1).astype(np.float32)


def spread_maps(xs, channels, x_major):
    rows_of, columns_of, masks = [], [], []
    lanes = xs * channels
    for start, (x_out, c_out) in zip(window_starts(lanes), column_map(xs, channels, x_major)):
        lane = start + np.arange(WINDOW)
        rows_of.append(lane[:, None] % channels == np.arange(channels)[None, :])
        columns_of.append(np.arange(channels)[:, None] == c_out[None, :])
        masks.append(band_masks(lane // channels, x_out))
    return [jnp.asarray(np.stack(m).astype(np.float32), BF16) for m in (rows_of, columns_of, masks)]


def first_maps(parts, xs, channels):
    row = np.arange(parts * xs)
    lane = np.arange(xs * channels)
    rows_of = row[:, None] // xs == np.arange(parts)[None, :]
    columns_of = np.arange(channels)[:, None] == lane[None, :] % channels
    masks = band_masks(row % xs, lane // channels)
    return [jnp.asarray(np.asarray(m, np.float32), BF16) for m in (rows_of, columns_of, masks)]


def spread_tap(kernel_ref, tap, rows_of, columns_of, masks):
    total = None
    for dx in range(3):
        tall = jnp.dot(rows_of, kernel_ref[tap, dx], preferred_element_type=F32).astype(BF16)
        wide = jnp.dot(tall, columns_of, preferred_element_type=F32)
        term = wide * masks[dx].astype(F32)
        total = term if total is None else total + term
    return total.astype(BF16)


def expand_kernel(
    y_here,
    k1_ref,
    k2_ref,
    k3_ref,
    r1_ref,
    c1_ref,
    m1_ref,
    r2_ref,
    c2_ref,
    m2_ref,
    r3_ref,
    c3_ref,
    m3_ref,
    w1_ref,
    side_ref,
    w2_ref,
    w3_ref,
):
    piece = r1_ref.shape[0]
    full = w1_ref.shape[1] // 3
    w1_ref[...] = jnp.zeros_like(w1_ref)
    side_ref[...] = jnp.zeros_like(side_ref)
    for dz in range(3):
        for dy in range(3):
            tap = dz * 3 + dy
            block = spread_tap(k1_ref, tap, r1_ref[...], c1_ref[...], m1_ref)
            for m in range(y_here):
                y = m + dy - 1
                if 0 <= y < y_here:
                    base = dz * full + y * piece
                    w1_ref[m, base : base + piece, :] = block
            if dy == 0:
                base = dz * full + (y_here - 1) * piece
                side_ref[0, base : base + piece, :] = block
            if dy == 2:
                side_ref[1, dz * full : dz * full + piece, :] = block

    def deep(tap, carry):
        base = pl.multiple_of(tap * WINDOW, WINDOW)
        for h in range(2):
            w2_ref[h, pl.ds(base, WINDOW), :] = spread_tap(
                k2_ref, tap, r2_ref[h], c2_ref[h], m2_ref.at[h]
            )
            w3_ref[h, pl.ds(base, WINDOW), :] = spread_tap(
                k3_ref, tap, r3_ref[h], c3_ref[h], m3_ref.at[h]
            )
        return carry

    lax.fori_loop(0, 9, deep, 0)


def expand_weights(first, second, third, y_here, xs):
    channels, parts = first.shape[:2]
    full = round_up(y_here * parts * xs, 128)
    lanes = xs * channels
    by_tap = [
        jnp.transpose(w, (2, 4, 3, 1, 0)).reshape(9, 3, w.shape[1], channels)
        for w in (first, second, third)
    ]
    maps = first_maps(parts, xs, channels)
    maps += spread_maps(xs, channels, True) + spread_maps(xs, channels, False)
    return pl.pallas_call(
        functools.partial(expand_kernel, y_here),
        out_shape=(
            jax.ShapeDtypeStruct((y_here, 3 * full, lanes), BF16),
            jax.ShapeDtypeStruct((2, 3 * full, lanes), BF16),
            jax.ShapeDtypeStruct((2, 9 * WINDOW, WINDOW), BF16),
            jax.ShapeDtypeStruct((2, 9 * WINDOW, xs // 2 * channels), BF16),
        ),
        in_specs=[vmem_spec()] * 12,
        out_specs=(vmem_spec(),) * 4,
        compiler_params=params(),
        cost_estimate=pl.CostEstimate(
            flops=20_000_000_000, bytes_accessed=10_000_000, transcendentals=0
        ),
    )(*by_tap, *maps)


def join(left, right):
    return jnp.concatenate(
        [left[:, :128], left[:, 128:] + right[:, :128], right[:, 128:]], axis=1
    )


def down_one(block):
    rolled = pltpu.roll(block, 1, 0)
    row = lax.broadcasted_iota(jnp.int32, block.shape, 0)
    return jnp.where(row == 0, 0.0, rolled)


def up_one(block):
    count = block.shape[0]
    rolled = pltpu.roll(block, count - 1, 0)
    row = lax.broadcasted_iota(jnp.int32, block.shape, 0)
    return jnp.where(row == count - 1, 0.0, rolled)


def net_kernel(
    place_ref,
    in_ref,
    w1_ref,
    w1_side_ref,
    w2_ref,
    w3_ref,
    b12_ref,
    b3_ref,
    order_ref,
    out_ref,
    spread,
    own,
    before,
    after,
    act1,
    act2,
):
    devices, rows_in, lanes_in = in_ref.shape
    z1, groups = act1.shape[:2]
    z2 = act2.shape[0]
    z_here = z2 - 2
    y_here = groups - 2
    first_z = place_ref[0]
    z_count = place_ref[1]
    window = 256
    lanes = act1.shape[3]

    def taps(act, z, h):
        start = h * (lanes - window)
        pieces = []
        for dz in range(3):
            for dy in range(3):
                piece = act[z + dz, dy : dy + y_here, :, start : start + window]
                pieces.append(piece.reshape(y_here * devices, window))
        return jnp.concatenate(pieces, axis=1)

    def inside(z):
        return jnp.where((z >= 0) & (z < z_count), 1.0, 0.0).astype(F32)

    @pl.when(pl.program_id(0) == 0)
    def _():
        for s in range(devices):
            piece = in_ref[s].astype(F32)
            for j in range(0, lanes_in, 128):
                spread[j // 128, pl.ds(s, rows_in, stride=devices), :] = piece[:, j : j + 128]

        tiles = [spread.at[j] for j in range(lanes_in // 128)]

        def shift(z, carry):
            base = pl.multiple_of(z * devices, devices)
            block = jnp.concatenate([part[pl.ds(base, devices), :] for part in tiles], axis=1)
            own[pl.ds(base, devices), :] = block.astype(BF16)
            before[pl.ds(base, devices), :] = down_one(block).astype(BF16)
            after[pl.ds(base, devices), :] = up_one(block).astype(BF16)
            return carry

        lax.fori_loop(0, z1 + 2, shift, 0)

        def first(z, carry):
            def three(ref):
                pieces = []
                for dz in range(3):
                    base = pl.multiple_of((z + dz) * devices, devices)
                    pieces.append(ref[pl.ds(base, devices), :])
                return jnp.concatenate(pieces, axis=1)

            mask = inside(first_z + z - 2)
            middle = three(own)
            for m in range(y_here):
                result = jnp.dot(middle, w1_ref[m], preferred_element_type=F32)
                if m == 0:
                    result += jnp.dot(three(before), w1_side_ref[0], preferred_element_type=F32)
                if m == y_here - 1:
                    result += jnp.dot(three(after), w1_side_ref[1], preferred_element_type=F32)
                value = jnp.maximum(result + b12_ref[0:1, :], 0.0) * mask
                act1[z, m + 1] = value.astype(BF16)
                if m == 0:
                    act1[z, groups - 1] = up_one(value).astype(BF16)
                if m == y_here - 1:
                    act1[z, 0] = down_one(value).astype(BF16)
            return carry

        lax.fori_loop(0, z1, first, 0)

        def second(z, carry):
            left = jnp.dot(taps(act1, z, 0), w2_ref[0], preferred_element_type=F32)
            right = jnp.dot(taps(act1, z, 1), w2_ref[1], preferred_element_type=F32)
            mask = inside(first_z + z - 1)
            value = jnp.maximum(join(left, right) + b12_ref[1:2, :], 0.0) * mask
            cube = value.reshape(y_here, devices, lanes)
            act2[z, 1 : groups - 1] = cube.astype(BF16)
            act2[z, groups - 1] = up_one(cube[0]).astype(BF16)
            act2[z, 0] = down_one(cube[y_here - 1]).astype(BF16)
            return carry

        lax.fori_loop(0, z2, second, 0)

    z = pl.program_id(0)
    channels, _, xs, y_count = out_ref.shape
    parts = []
    for h in range(2):
        result = jnp.dot(taps(act2, z, h), w3_ref[h], preferred_element_type=F32)
        value = jnp.maximum(result + b3_ref[...], 0.0).astype(BF16)
        turned = lax.dot_general(
            value, order_ref[...], (((0,), (0,)), ((), ())), preferred_element_type=F32
        )
        parts.append(turned.reshape(channels, xs // 2, y_count))
    out_ref[:, 0] = jnp.concatenate(parts, axis=1).astype(BF16)


def network(gathered, place, weights, biases, z_here, xs, y_here):
    devices, rows_in, lanes_in = gathered.shape
    channels = biases[0].shape[0]
    y_count = y_here * devices
    lanes = xs * channels
    w1, w1_side, w2, w3 = weights
    b12 = jnp.stack([jnp.tile(biases[0], xs), jnp.tile(biases[1], xs)])
    b3 = jnp.repeat(biases[2], xs // 2)[None]
    row = np.arange(y_count)
    order = np.zeros((y_count, y_count), np.float32)
    order[row, row % devices * y_here + row // devices] = 1.0
    order = jnp.asarray(order, BF16)
    z1, z2 = z_here + 4, z_here + 2
    groups = y_here + 2
    return pl.pallas_call(
        net_kernel,
        out_shape=jax.ShapeDtypeStruct((channels, z_here, xs, y_count), BF16),
        grid=(z_here,),
        in_specs=[pl.BlockSpec(memory_space=pltpu.SMEM)] + [vmem_spec()] * 8,
        out_specs=pl.BlockSpec((channels, 1, xs, y_count), lambda z: (0, z, 0, 0)),
        scratch_shapes=[
            pltpu.VMEM((lanes_in // 128, rows_in * devices, 128), F32),
            pltpu.VMEM((rows_in * devices, lanes_in), BF16),
            pltpu.VMEM((rows_in * devices, lanes_in), BF16),
            pltpu.VMEM((rows_in * devices, lanes_in), BF16),
            pltpu.VMEM((z1, groups, devices, lanes), BF16),
            pltpu.VMEM((z2, groups, devices, lanes), BF16),
        ],
        compiler_params=params(),
    )(place, gathered, w1, w1_side, w2, w3, b12, b3, order)


def on_device(
    kspace,
    sensitivity,
    weight_first,
    bias_first,
    weight_second,
    bias_second,
    weight_third,
    bias_third,
):
    devices = lax.axis_size("kz")
    _, y_here, _, xs, z_count = sensitivity.shape
    z_here = z_count // devices
    lines = y_transform(kspace, devices)
    received = lax.all_to_all(lines, "kz", 0, 0)
    weights = expand_weights(weight_first, weight_second, weight_third, y_here, xs)
    received, weights = lax.optimization_barrier((received, weights))
    merged = z_transform(received, sensitivity, devices)
    gathered = lax.all_to_all(merged, "kz", 0, 0)
    place = jnp.stack([lax.axis_index("kz") * z_here, z_count]).astype(jnp.int32)
    biases = (bias_first, bias_second, bias_third)
    return network(gathered, place, weights, biases, z_here, xs, y_here)


def solution(mesh):
    in_specs = (
        P("grp", None, "kz", None),
        P(None, ("grp", "kz"), None, None, None),
        P(),
        P(),
        P(),
        P(),
        P(),
        P(),
    )
    out_specs = P("grp", "kz", None, None)
    return jax.shard_map(
        on_device, mesh=mesh, in_specs=in_specs, out_specs=out_specs, check_vma=False
    )
```

```python
import functools
import math

import jax
import jax.numpy as jnp
import numpy as np
from jax import lax
from jax.experimental import pallas as pl
from jax.experimental.pallas import tpu as pltpu
from jax.sharding import PartitionSpec as P

BF16 = jnp.bfloat16
F32 = jnp.float32
HALO = 3
WINDOW = 256
Y_GROUP = 4
Y_PASSES = 2
Z_PASSES = 1
Z_WIDTH = 256
SECOND_GROUP = 3
THIRD_GROUP = 4
VMEM_LIMIT = 56 * 1024 * 1024


def round_up(value, unit):
    return -(-value // unit) * unit


def params():
    return pltpu.CompilerParams(vmem_limit_bytes=VMEM_LIMIT)


def vmem_spec():
    return pl.BlockSpec(memory_space=pltpu.VMEM)


def halves(table):
    high = table.astype(jnp.bfloat16)
    low = (table - high.astype(np.float64)).astype(jnp.bfloat16)
    return high, low


def trig(length, rows, cols):
    phase = (rows[:, None] * cols[None, :]) % length
    angle = phase * (2.0 * math.pi / length)
    return np.cos(angle), np.sin(angle)


def y_table(y_count, devices):
    y_here = y_count // devices
    order = (np.arange(devices)[None, :] * y_here + np.arange(y_here)[:, None]).reshape(-1)
    cosine, sine = trig(y_count, order, np.arange(y_count))
    real = np.concatenate([cosine, -sine], axis=1)
    imag = np.concatenate([sine, cosine], axis=1)
    table = np.stack([real, imag], axis=1).reshape(2 * y_count, 2 * y_count)
    return table / math.sqrt(y_count)


def z_table(z_count, devices):
    cosine, sine = trig(z_count, np.arange(z_count), np.arange(z_count))
    real = np.concatenate([cosine, sine], axis=1)
    imag = np.concatenate([-sine, cosine], axis=1)
    table = np.stack([real, imag], axis=0).reshape(2, devices, z_count // devices, 2 * z_count)
    return np.transpose(table, (1, 0, 2, 3)).reshape(2 * z_count, 2 * z_count)


def y_kernel(devices, k_ref, t_ref, out_ref, lines, turned, sems):
    kz_here, pairs, _ = lines.shape
    rows = t_ref.shape[0]
    group = Y_GROUP

    def fetch(kz):
        return pltpu.make_async_copy(k_ref.at[:, kz, :], lines.at[kz], sems.at[kz])

    for kz in range(kz_here):
        fetch(kz).start()
    for first in range(0, kz_here, group):
        for kz in range(first, first + group):
            fetch(kz).wait()
        line = lines[first : first + group].reshape(group * pairs, lines.shape[2])
        high = line.astype(BF16)
        terms = [high]
        if Y_PASSES > 1:
            terms.append(high)
        if Y_PASSES > 2:
            terms.append((line - high.astype(F32)).astype(BF16))
        operand = jnp.concatenate(terms, axis=1)
        result = lax.dot_general(
            t_ref[...], operand, (((1,), (1,)), ((), ())), preferred_element_type=F32
        )
        for i in range(group):
            turned[pl.ds(first + i, rows, stride=kz_here), :] = result[
                :, i * pairs : (i + 1) * pairs
            ]
    block = 2 * kz_here
    for row in range(rows // 2):
        y, device = row // devices, row % devices
        out_ref[device, :, y * pairs : (y + 1) * pairs] = turned[
            row * block : (row + 1) * block, :
        ].astype(BF16)


def y_transform(kspace, devices):
    coils, xs, kz_here, width = kspace.shape
    pairs = coils * xs
    y_count = width // 2
    high, low = halves(y_table(y_count, devices))
    table = jnp.asarray(np.concatenate([high, low, high][:Y_PASSES], axis=1))
    return pl.pallas_call(
        functools.partial(y_kernel, devices),
        out_shape=jax.ShapeDtypeStruct((devices, 2 * kz_here, y_count // devices * pairs), BF16),
        in_specs=[pl.BlockSpec(memory_space=pl.ANY), vmem_spec()],
        out_specs=vmem_spec(),
        scratch_shapes=[
            pltpu.VMEM((kz_here, pairs, width), F32),
            pltpu.VMEM((2 * y_count * kz_here, pairs), F32),
            pltpu.SemaphoreType.DMA((kz_here,)),
        ],
        compiler_params=params(),
    )(kspace.reshape(pairs, kz_here, width), table)


def z_kernel(scale, devices, z_here, r_ref, t_ref, s_ref, out_ref, lines, turned):
    step = pl.program_id(0)
    _, y_here, coils, xs, width = s_ref.shape
    lanes = out_ref.shape[2]

    @pl.when(step == 0)
    def _():
        lines[...] = r_ref[...].T
        turned[...] = jnp.zeros_like(turned)

    operand = lines[...]
    if Z_PASSES > 1:
        operand = jnp.concatenate([operand, operand], axis=1)
    images = jnp.dot(operand, t_ref[0], preferred_element_type=F32)
    image_re = images[:, :width].reshape(y_here, coils, xs, width)
    image_im = images[:, width:].reshape(y_here, coils, xs, width)
    sens_re = s_ref[0]
    sens_im = s_ref[1]
    real = jnp.sum(sens_re * image_re + sens_im * image_im, axis=1) * scale
    imag = jnp.sum(sens_re * image_im - sens_im * image_re, axis=1) * scale
    merged = jnp.concatenate([real, imag], axis=1).reshape(y_here * 2 * xs, width)
    if lanes > y_here * 2 * xs:
        merged = jnp.concatenate([merged, jnp.zeros((lanes - y_here * 2 * xs, width), F32)], axis=0)
    base = pl.multiple_of(8 + step * width, 8)
    turned[pl.ds(base, width), :] = merged.T

    @pl.when(step == pl.num_programs(0) - 1)
    def _():
        rows = out_ref.shape[1]
        for device in range(devices):
            first = 8 + device * z_here - HALO
            out_ref[device] = turned[first : first + rows, :].astype(BF16)


def z_transform(received, sensitivity, devices):
    _, y_here, coils, xs, z_count = sensitivity.shape
    pairs = coils * xs
    width = Z_WIDTH
    high, low = halves(z_table(z_count, devices))
    table = np.concatenate([high, low][:Z_PASSES], axis=0)
    depth = table.shape[0]
    table = table.reshape(depth, 2, z_count // width, width).transpose(2, 0, 1, 3)
    table = jnp.asarray(table.reshape(z_count // width, depth, 2 * width))
    scale = 1.0 / math.sqrt(z_count)
    rows = round_up(z_count // devices + 2 * HALO, 8)
    lanes = round_up(y_here * 2 * xs, 128)
    flat = received.reshape(2 * z_count, y_here * pairs)
    return pl.pallas_call(
        functools.partial(z_kernel, scale, devices, z_count // devices),
        out_shape=jax.ShapeDtypeStruct((devices, rows, lanes), BF16),
        grid=(z_count // width,),
        in_specs=[
            pl.BlockSpec(flat.shape, lambda z: (0, 0)),
            pl.BlockSpec((1, depth, 2 * width), lambda z: (z, 0, 0)),
            pl.BlockSpec((2, y_here, coils, xs, width), lambda z: (0, 0, 0, 0, z)),
        ],
        out_specs=pl.BlockSpec((devices, rows, lanes), lambda z: (0, 0, 0)),
        scratch_shapes=[
            pltpu.VMEM(flat.shape[::-1], BF16),
            pltpu.VMEM((8 + z_count + 32, lanes), F32),
        ],
        compiler_params=params(),
    )(flat, table, sensitivity)


def window_starts(lanes):
    return (0, lanes - WINDOW)


def column_map(xs, channels, x_major):
    half = xs // 2
    found = []
    for h in range(2):
        x, c = np.meshgrid(np.arange(half) + h * half, np.arange(channels), indexing="ij")
        if x_major:
            pad = np.full(WINDOW - half * channels, -9)
            x, c = x.reshape(-1), c.reshape(-1)
            order = [(pad, x), (pad, c)] if h else [(x, pad), (c, pad)]
            found.append((np.concatenate(order[0]), np.concatenate(order[1])))
        else:
            found.append((x.T.reshape(-1), c.T.reshape(-1)))
    return found


def band_masks(x_in, x_out):
    taps = np.arange(3)[:, None, None]
    return (x_in[None, :, None] == x_out[None, None, :] + taps - 1).astype(np.float32)


def spread_maps(xs, channels, x_major):
    rows_of, columns_of, masks = [], [], []
    lanes = xs * channels
    for start, (x_out, c_out) in zip(window_starts(lanes), column_map(xs, channels, x_major)):
        lane = start + np.arange(WINDOW)
        rows_of.append(lane[:, None] % channels == np.arange(channels)[None, :])
        columns_of.append(np.arange(channels)[:, None] == c_out[None, :])
        masks.append(band_masks(lane // channels, x_out))
    return [jnp.asarray(np.stack(m).astype(np.float32), BF16) for m in (rows_of, columns_of, masks)]


def first_maps(parts, xs, channels):
    row = np.arange(parts * xs)
    lane = np.arange(xs * channels)
    rows_of = row[:, None] // xs == np.arange(parts)[None, :]
    columns_of = np.arange(channels)[:, None] == lane[None, :] % channels
    masks = band_masks(row % xs, lane // channels)
    return [jnp.asarray(np.asarray(m, np.float32), BF16) for m in (rows_of, columns_of, masks)]


def spread_tap(kernel_ref, tap, rows_of, columns_of, masks):
    total = None
    for dx in range(3):
        tall = jnp.dot(rows_of, kernel_ref[tap, dx], preferred_element_type=F32).astype(BF16)
        wide = jnp.dot(tall, columns_of, preferred_element_type=F32)
        term = wide * masks[dx].astype(F32)
        total = term if total is None else total + term
    return total.astype(BF16)


def expand_kernel(
    y_here,
    k1_ref,
    k2_ref,
    k3_ref,
    r1_ref,
    c1_ref,
    m1_ref,
    r2_ref,
    c2_ref,
    m2_ref,
    r3_ref,
    c3_ref,
    m3_ref,
    w1_ref,
    side_ref,
    w2_ref,
    w3_ref,
):
    piece = r1_ref.shape[0]
    full = w1_ref.shape[1] // 3
    w1_ref[...] = jnp.zeros_like(w1_ref)
    side_ref[...] = jnp.zeros_like(side_ref)
    for dz in range(3):
        for dy in range(3):
            tap = dz * 3 + dy
            block = spread_tap(k1_ref, tap, r1_ref[...], c1_ref[...], m1_ref)
            for m in range(y_here):
                y = m + dy - 1
                if 0 <= y < y_here:
                    base = dz * full + y * piece
                    w1_ref[m, base : base + piece, :] = block
            if dy == 0:
                base = dz * full + (y_here - 1) * piece
                side_ref[0, base : base + piece, :] = block
            if dy == 2:
                side_ref[1, dz * full : dz * full + piece, :] = block

    def deep(tap, carry):
        base = pl.multiple_of(tap * WINDOW, WINDOW)
        for h in range(2):
            w2_ref[h, pl.ds(base, WINDOW), :] = spread_tap(
                k2_ref, tap, r2_ref[h], c2_ref[h], m2_ref.at[h]
            )
            w3_ref[h, pl.ds(base, WINDOW), :] = spread_tap(
                k3_ref, tap, r3_ref[h], c3_ref[h], m3_ref.at[h]
            )
        return carry

    lax.fori_loop(0, 9, deep, 0)


def expand_weights(first, second, third, y_here, xs):
    channels, parts = first.shape[:2]
    full = round_up(y_here * parts * xs, 128)
    lanes = xs * channels
    by_tap = [
        jnp.transpose(w, (2, 4, 3, 1, 0)).reshape(9, 3, w.shape[1], channels)
        for w in (first, second, third)
    ]
    maps = first_maps(parts, xs, channels)
    maps += spread_maps(xs, channels, True) + spread_maps(xs, channels, False)
    return pl.pallas_call(
        functools.partial(expand_kernel, y_here),
        out_shape=(
            jax.ShapeDtypeStruct((y_here, 3 * full, lanes), BF16),
            jax.ShapeDtypeStruct((2, 3 * full, lanes), BF16),
            jax.ShapeDtypeStruct((2, 9 * WINDOW, WINDOW), BF16),
            jax.ShapeDtypeStruct((2, 9 * WINDOW, xs // 2 * channels), BF16),
        ),
        in_specs=[vmem_spec()] * 12,
        out_specs=(vmem_spec(),) * 4,
        compiler_params=params(),
        cost_estimate=pl.CostEstimate(
            flops=20_000_000_000, bytes_accessed=10_000_000, transcendentals=0
        ),
    )(*by_tap, *maps)


def join(left, right):
    return jnp.concatenate(
        [left[:, :128], left[:, 128:] + right[:, :128], right[:, 128:]], axis=1
    )


def down_one(block):
    rolled = pltpu.roll(block, 1, 0)
    row = lax.broadcasted_iota(jnp.int32, block.shape, 0)
    return jnp.where(row == 0, 0.0, rolled)


def up_one(block):
    count = block.shape[0]
    rolled = pltpu.roll(block, count - 1, 0)
    row = lax.broadcasted_iota(jnp.int32, block.shape, 0)
    return jnp.where(row == count - 1, 0.0, rolled)


def net_kernel(
    place_ref,
    in_ref,
    w1_ref,
    w1_side_ref,
    w2_ref,
    w3_ref,
    b12_ref,
    b3_ref,
    order_ref,
    out_ref,
    spread,
    own,
    before,
    after,
    act1,
    act2,
):
    devices, rows_in, lanes_in = in_ref.shape
    z1, groups = act1.shape[:2]
    z2 = act2.shape[0]
    z_here = z2 - 2
    y_here = groups - 2
    first_z = place_ref[0]
    z_count = place_ref[1]
    window = 256
    lanes = act1.shape[3]

    def taps(act, z, count, h):
        start = h * (lanes - window)
        pieces = []
        for dz in range(3):
            for dy in range(3):
                piece = act[pl.ds(z + dz, count), dy : dy + y_here, :, start : start + window]
                pieces.append(piece.reshape(count * y_here * devices, window))
        return jnp.concatenate(pieces, axis=1)

    @pl.when(pl.program_id(0) == 0)
    def _():
        for s in range(devices):
            piece = in_ref[s].astype(F32)
            for j in range(0, lanes_in, 128):
                spread[j // 128, pl.ds(s, rows_in, stride=devices), :] = piece[:, j : j + 128]

        tiles = [spread.at[j] for j in range(lanes_in // 128)]

        def shift(z, carry):
            base = pl.multiple_of(z * devices, devices)
            block = jnp.concatenate([part[pl.ds(base, devices), :] for part in tiles], axis=1)
            own[pl.ds(base, devices), :] = block.astype(BF16)
            before[pl.ds(base, devices), :] = down_one(block).astype(BF16)
            after[pl.ds(base, devices), :] = up_one(block).astype(BF16)
            return carry

        lax.fori_loop(0, z1 + 2, shift, 0)

        def three(ref):
            count = z1 * devices
            return jnp.concatenate(
                [ref[dz * devices : dz * devices + count, :] for dz in range(3)], axis=1
            )

        for m in range(y_here):
            result = jnp.dot(three(own), w1_ref[m], preferred_element_type=F32)
            if m == 0:
                result += jnp.dot(three(before), w1_side_ref[0], preferred_element_type=F32)
            if m == y_here - 1:
                result += jnp.dot(three(after), w1_side_ref[1], preferred_element_type=F32)
            value = jnp.maximum(result + b12_ref[0:1, :], 0.0).reshape(z1, devices, lanes)
            act1[:, m + 1] = value.astype(BF16)
            for z in range(z1):
                if m == 0:
                    act1[z, groups - 1] = up_one(value[z]).astype(BF16)
                if m == y_here - 1:
                    act1[z, 0] = down_one(value[z]).astype(BF16)
        for z in (0, 1, z1 - 2, z1 - 1):
            here = first_z + z - 2

            @pl.when((here < 0) | (here >= z_count))
            def _():
                act1[z] = jnp.zeros_like(act1[z])

        many = SECOND_GROUP

        def second(step, carry):
            z = step * many
            left = jnp.dot(taps(act1, z, many, 0), w2_ref[0], preferred_element_type=F32)
            right = jnp.dot(taps(act1, z, many, 1), w2_ref[1], preferred_element_type=F32)
            value = jnp.maximum(join(left, right) + b12_ref[1:2, :], 0.0)
            cube = value.reshape(many, y_here, devices, lanes)
            act2[pl.ds(z, many), 1 : groups - 1] = cube.astype(BF16)
            for i in range(many):
                act2[z + i, groups - 1] = up_one(cube[i, 0]).astype(BF16)
                act2[z + i, 0] = down_one(cube[i, y_here - 1]).astype(BF16)
            return carry

        lax.fori_loop(0, z2 // many, second, 0)
        for z in (0, z2 - 1):
            here = first_z + z - 1

            @pl.when((here < 0) | (here >= z_count))
            def _():
                act2[z] = jnp.zeros_like(act2[z])

    channels, many, xs, y_count = out_ref.shape
    z = pl.program_id(0) * many
    parts = []
    for h in range(2):
        result = jnp.dot(taps(act2, z, many, h), w3_ref[h], preferred_element_type=F32)
        value = jnp.maximum(result + b3_ref[...], 0.0).astype(BF16)
        parts.append(value)
    for i in range(many):
        pieces = []
        for value in parts:
            turned = lax.dot_general(
                value[i * y_count : (i + 1) * y_count],
                order_ref[...],
                (((0,), (0,)), ((), ())),
                preferred_element_type=F32,
            )
            pieces.append(turned.reshape(channels, xs // 2, y_count))
        out_ref[:, i] = jnp.concatenate(pieces, axis=1).astype(BF16)


def network(gathered, place, weights, biases, z_here, xs, y_here):
    devices, rows_in, lanes_in = gathered.shape
    channels = biases[0].shape[0]
    y_count = y_here * devices
    lanes = xs * channels
    w1, w1_side, w2, w3 = weights
    b12 = jnp.stack([jnp.tile(biases[0], xs), jnp.tile(biases[1], xs)])
    b3 = jnp.repeat(biases[2], xs // 2)[None]
    row = np.arange(y_count)
    order = np.zeros((y_count, y_count), np.float32)
    order[row, row % devices * y_here + row // devices] = 1.0
    order = jnp.asarray(order, BF16)
    z1, z2 = z_here + 4, z_here + 2
    groups = y_here + 2
    return pl.pallas_call(
        net_kernel,
        out_shape=jax.ShapeDtypeStruct((channels, z_here, xs, y_count), BF16),
        grid=(z_here // THIRD_GROUP,),
        in_specs=[pl.BlockSpec(memory_space=pltpu.SMEM)] + [vmem_spec()] * 8,
        out_specs=pl.BlockSpec((channels, THIRD_GROUP, xs, y_count), lambda z: (0, z, 0, 0)),
        scratch_shapes=[
            pltpu.VMEM((lanes_in // 128, rows_in * devices, 128), F32),
            pltpu.VMEM((rows_in * devices, lanes_in), BF16),
            pltpu.VMEM((rows_in * devices, lanes_in), BF16),
            pltpu.VMEM((rows_in * devices, lanes_in), BF16),
            pltpu.VMEM((z1, groups, devices, lanes), BF16),
            pltpu.VMEM((z2, groups, devices, lanes), BF16),
        ],
        compiler_params=params(),
    )(place, gathered, w1, w1_side, w2, w3, b12, b3, order)


def on_device(
    kspace,
    sensitivity,
    weight_first,
    bias_first,
    weight_second,
    bias_second,
    weight_third,
    bias_third,
):
    devices = lax.axis_size("kz")
    _, y_here, _, xs, z_count = sensitivity.shape
    z_here = z_count // devices
    lines = y_transform(kspace, devices)
    received = lax.all_to_all(lines, "kz", 0, 0)
    weights = expand_weights(weight_first, weight_second, weight_third, y_here, xs)
    received, weights = lax.optimization_barrier((received, weights))
    merged = z_transform(received, sensitivity, devices)
    gathered = lax.all_to_all(merged, "kz", 0, 0)
    place = jnp.stack([lax.axis_index("kz") * z_here, z_count]).astype(jnp.int32)
    biases = (bias_first, bias_second, bias_third)
    return network(gathered, place, weights, biases, z_here, xs, y_here)


def solution(mesh):
    in_specs = (
        P("grp", None, "kz", None),
        P(None, ("grp", "kz"), None, None, None),
        P(),
        P(),
        P(),
        P(),
        P(),
        P(),
    )
    out_specs = P("grp", "kz", None, None)
    return jax.shard_map(
        on_device, mesh=mesh, in_specs=in_specs, out_specs=out_specs, check_vma=False
    )
```

```python
import functools
import math

import jax
import jax.numpy as jnp
import numpy as np
from jax import lax
from jax.experimental import pallas as pl
from jax.experimental.pallas import tpu as pltpu
from jax.sharding import PartitionSpec as P

BF16 = jnp.bfloat16
F32 = jnp.float32
HALO = 3
WINDOW = 256
Y_GROUP = 4
Y_PASSES = 3
Z_WIDTH = 128
CODE_SCALE = 2.0**20
SECOND_GROUP = 3
THIRD_GROUP = 4
VMEM_LIMIT = 56 * 1024 * 1024


def round_up(value, unit):
    return -(-value // unit) * unit


def params():
    return pltpu.CompilerParams(vmem_limit_bytes=VMEM_LIMIT)


def vmem_spec():
    return pl.BlockSpec(memory_space=pltpu.VMEM)


def halves(table):
    high = table.astype(jnp.bfloat16)
    low = (table - high.astype(np.float64)).astype(jnp.bfloat16)
    return high, low


def trig(length, rows, cols):
    phase = (rows[:, None] * cols[None, :]) % length
    angle = phase * (2.0 * math.pi / length)
    return np.cos(angle), np.sin(angle)


def parities(kz_here):
    return 2 if kz_here % 16 == 0 else 1


def y_table(y_count, devices):
    y_here = y_count // devices
    order = (np.arange(devices)[None, :] * y_here + np.arange(y_here)[:, None]).reshape(-1)
    cosine, sine = trig(y_count, order, np.arange(y_count))
    real = np.concatenate([cosine, -sine], axis=1)
    imag = np.concatenate([sine, cosine], axis=1)
    return np.concatenate([real, imag], axis=0) * (CODE_SCALE / math.sqrt(y_count))


def z_table(z_count, devices, groups, width):
    kz_here = z_count // devices
    outputs = z_count // groups
    tables = []
    for parity in range(groups):
        kz = np.arange(devices)[:, None] * kz_here + np.arange(parity, kz_here, groups)[None, :]
        cosine, sine = trig(z_count, kz.reshape(-1), np.arange(outputs))
        both = np.stack([np.stack([cosine, sine], 1), np.stack([-sine, cosine], 1)], 0)
        both = both.reshape(2, devices, kz_here // groups, 2, outputs // width, width)
        both = both.transpose(4, 1, 0, 2, 3, 5)
        tables.append(both.reshape(outputs // width, 2 * z_count // groups, 2 * width))
    return np.stack(tables)


def encode(value):
    square = value * jnp.abs(value)
    return (square * jnp.abs(square)).astype(BF16)


def decode(code):
    code = code.astype(F32)
    root = jnp.sqrt(jnp.sqrt(jnp.abs(code)))
    return jnp.where(code < 0, -root, root)


def y_kernel(devices, k_ref, t_ref, out_ref, lines, turned, sems):
    kz_here, pairs, _ = lines.shape
    rows = t_ref.shape[0]
    group = min(Y_GROUP, kz_here)
    groups = parities(kz_here)

    def fetch(kz):
        return pltpu.make_async_copy(k_ref.at[:, kz, :], lines.at[kz], sems.at[kz])

    for kz in range(kz_here):
        fetch(kz).start()
    for first in range(0, kz_here, group):
        for kz in range(first, first + group):
            fetch(kz).wait()
        line = lines[first : first + group].reshape(group * pairs, lines.shape[2])
        high = line.astype(BF16)
        terms = [high]
        if Y_PASSES > 1:
            terms.append(high)
        if Y_PASSES > 2:
            terms.append((line - high.astype(F32)).astype(BF16))
        operand = jnp.concatenate(terms, axis=1)
        result = lax.dot_general(
            t_ref[...], operand, (((1,), (1,)), ((), ())), preferred_element_type=F32
        )
        block = 2 * kz_here
        half = rows // 2
        for i in range(group):
            kz = first + i
            for part in range(2):
                place = kz % groups * (block // groups)
                place += part * (kz_here // groups) + kz // groups
                turned[pl.ds(place, half, stride=block), :] = result[
                    part * half : (part + 1) * half, i * pairs : (i + 1) * pairs
                ]
    for row in range(rows // 2):
        y, device = row // devices, row % devices
        out_ref[device, :, y * pairs : (y + 1) * pairs] = encode(
            turned[row * block : (row + 1) * block, :]
        )


def y_transform(kspace, devices):
    coils, xs, kz_here, width = kspace.shape
    pairs = coils * xs
    y_count = width // 2
    high, low = halves(y_table(y_count, devices))
    table = jnp.asarray(np.concatenate([high, low, high][:Y_PASSES], axis=1))
    return pl.pallas_call(
        functools.partial(y_kernel, devices),
        out_shape=jax.ShapeDtypeStruct((devices, 2 * kz_here, y_count // devices * pairs), BF16),
        in_specs=[pl.BlockSpec(memory_space=pl.ANY), vmem_spec()],
        out_specs=vmem_spec(),
        scratch_shapes=[
            pltpu.VMEM((kz_here, pairs, width), F32),
            pltpu.VMEM((2 * y_count * kz_here, pairs), F32),
            pltpu.SemaphoreType.DMA((kz_here,)),
        ],
        compiler_params=params(),
    )(kspace.reshape(pairs, kz_here, width), table)


def z_kernel(scale, devices, z_here, groups, r_ref, t_ref, *refs):
    s_refs, out_ref, codes, lines, turned = refs[:groups], *refs[groups:]
    step = pl.program_id(0)
    _, y_here, coils, xs, width = s_refs[0].shape
    lanes = out_ref.shape[2]
    columns = r_ref.shape[2]
    rows = r_ref.shape[1] // groups
    depth = devices * rows

    @pl.when(step == 0)
    def _():
        for parity in range(groups):
            piece = r_ref[:, parity * rows : (parity + 1) * rows, :]
            codes[parity] = piece.reshape(depth, columns).T
        turned[...] = jnp.zeros_like(turned)

        def unpack(i, carry):
            at = pl.ds(pl.multiple_of(i * 32, 32), 32)
            for parity in range(groups):
                value = decode(codes[parity, at, :])
                high = value.astype(BF16)
                lines[parity, at, :depth] = high
                lines[parity, at, depth:] = (value - high.astype(F32)).astype(BF16)
            return carry

        lax.fori_loop(0, columns // 32, unpack, 0)

    products = []
    for parity in range(groups):
        operand = lines[parity]
        operand = jnp.concatenate([operand, operand[:, :depth]], axis=1)
        products.append(jnp.dot(operand, t_ref[parity, 0], preferred_element_type=F32))
    if groups == 2:
        products = [products[0] + products[1], products[0] - products[1]]
    for part, (images, s_ref) in enumerate(zip(products, s_refs)):
        image_re = images[:, :width].reshape(y_here, coils, xs, width)
        image_im = images[:, width:].reshape(y_here, coils, xs, width)
        sens_re = s_ref[0]
        sens_im = s_ref[1]
        real = jnp.sum(sens_re * image_re + sens_im * image_im, axis=1) * scale
        imag = jnp.sum(sens_re * image_im - sens_im * image_re, axis=1) * scale
        merged = jnp.concatenate([real, imag], axis=1).reshape(y_here * 2 * xs, width)
        extra = lanes - y_here * 2 * xs
        if extra:
            merged = jnp.concatenate([merged, jnp.zeros((extra, width), F32)], axis=0)
        base = 8 + part * devices * z_here // groups
        base = pl.multiple_of(base + step * width, 8)
        turned[pl.ds(base, width), :] = merged.T

    @pl.when(step == pl.num_programs(0) - 1)
    def _():
        for device in range(devices):
            first = 8 + device * z_here - HALO
            out_ref[device] = turned[first : first + out_ref.shape[1], :].astype(BF16)


def z_transform(received, sensitivity, devices):
    _, y_here, coils, xs, z_count = sensitivity.shape
    pairs = coils * xs
    width = Z_WIDTH
    groups = parities(z_count // devices)
    high, low = halves(z_table(z_count, devices, groups, width))
    table = jnp.asarray(np.concatenate([high, high, low], axis=2))
    scale = 1.0 / (math.sqrt(z_count) * CODE_SCALE)
    rows = round_up(z_count // devices + 2 * HALO, 8)
    lanes = round_up(y_here * 2 * xs, 128)
    steps = z_count // groups // width
    depth = 2 * z_count // groups

    def sens_spec(part):
        return pl.BlockSpec(
            (2, y_here, coils, xs, width), lambda z: (0, 0, 0, 0, z + part * steps)
        )

    return pl.pallas_call(
        functools.partial(z_kernel, scale, devices, z_count // devices, groups),
        out_shape=jax.ShapeDtypeStruct((devices, rows, lanes), BF16),
        grid=(steps,),
        in_specs=[
            pl.BlockSpec(received.shape, lambda z: (0, 0, 0)),
            pl.BlockSpec((groups, 1, 3 * depth, 2 * width), lambda z: (0, z, 0, 0)),
        ]
        + [sens_spec(part) for part in range(groups)],
        out_specs=pl.BlockSpec((devices, rows, lanes), lambda z: (0, 0, 0)),
        scratch_shapes=[
            pltpu.VMEM((groups, y_here * pairs, depth), BF16),
            pltpu.VMEM((groups, y_here * pairs, 2 * depth), BF16),
            pltpu.VMEM((8 + z_count + 32, lanes), F32),
        ],
        compiler_params=params(),
    )(received, table, *[sensitivity] * groups)


def window_starts(lanes):
    return (0, lanes - WINDOW)


def column_map(xs, channels, x_major):
    half = xs // 2
    found = []
    for h in range(2):
        x, c = np.meshgrid(np.arange(half) + h * half, np.arange(channels), indexing="ij")
        if x_major:
            pad = np.full(WINDOW - half * channels, -9)
            x, c = x.reshape(-1), c.reshape(-1)
            order = [(pad, x), (pad, c)] if h else [(x, pad), (c, pad)]
            found.append((np.concatenate(order[0]), np.concatenate(order[1])))
        else:
            found.append((x.T.reshape(-1), c.T.reshape(-1)))
    return found


def band_masks(x_in, x_out):
    taps = np.arange(3)[:, None, None]
    return (x_in[None, :, None] == x_out[None, None, :] + taps - 1).astype(np.float32)


def spread_maps(xs, channels, x_major):
    rows_of, columns_of, masks = [], [], []
    lanes = xs * channels
    for start, (x_out, c_out) in zip(window_starts(lanes), column_map(xs, channels, x_major)):
        lane = start + np.arange(WINDOW)
        rows_of.append(lane[:, None] % channels == np.arange(channels)[None, :])
        columns_of.append(np.arange(channels)[:, None] == c_out[None, :])
        masks.append(band_masks(lane // channels, x_out))
    return [jnp.asarray(np.stack(m).astype(np.float32), BF16) for m in (rows_of, columns_of, masks)]


def first_maps(parts, xs, channels):
    row = np.arange(parts * xs)
    lane = np.arange(xs * channels)
    rows_of = row[:, None] // xs == np.arange(parts)[None, :]
    columns_of = np.arange(channels)[:, None] == lane[None, :] % channels
    masks = band_masks(row % xs, lane // channels)
    return [jnp.asarray(np.asarray(m, np.float32), BF16) for m in (rows_of, columns_of, masks)]


def spread_tap(kernel_ref, tap, rows_of, columns_of, masks):
    total = None
    for dx in range(3):
        tall = jnp.dot(rows_of, kernel_ref[tap, dx], preferred_element_type=F32).astype(BF16)
        wide = jnp.dot(tall, columns_of, preferred_element_type=F32)
        term = wide * masks[dx].astype(F32)
        total = term if total is None else total + term
    return total.astype(BF16)


def expand_kernel(
    y_here,
    k1_ref,
    k2_ref,
    k3_ref,
    r1_ref,
    c1_ref,
    m1_ref,
    r2_ref,
    c2_ref,
    m2_ref,
    r3_ref,
    c3_ref,
    m3_ref,
    w1_ref,
    side_ref,
    w2_ref,
    w3_ref,
):
    piece = r1_ref.shape[0]
    full = w1_ref.shape[1] // 3
    w1_ref[...] = jnp.zeros_like(w1_ref)
    side_ref[...] = jnp.zeros_like(side_ref)
    for dz in range(3):
        for dy in range(3):
            tap = dz * 3 + dy
            block = spread_tap(k1_ref, tap, r1_ref[...], c1_ref[...], m1_ref)
            for m in range(y_here):
                y = m + dy - 1
                if 0 <= y < y_here:
                    base = dz * full + y * piece
                    w1_ref[m, base : base + piece, :] = block
            if dy == 0:
                base = dz * full + (y_here - 1) * piece
                side_ref[0, base : base + piece, :] = block
            if dy == 2:
                side_ref[1, dz * full : dz * full + piece, :] = block

    def deep(tap, carry):
        base = pl.multiple_of(tap * WINDOW, WINDOW)
        for h in range(2):
            w2_ref[h, pl.ds(base, WINDOW), :] = spread_tap(
                k2_ref, tap, r2_ref[h], c2_ref[h], m2_ref.at[h]
            )
            w3_ref[h, pl.ds(base, WINDOW), :] = spread_tap(
                k3_ref, tap, r3_ref[h], c3_ref[h], m3_ref.at[h]
            )
        return carry

    lax.fori_loop(0, 9, deep, 0)


def expand_weights(first, second, third, y_here, xs):
    channels, parts = first.shape[:2]
    full = round_up(y_here * parts * xs, 128)
    lanes = xs * channels
    by_tap = [
        jnp.transpose(w, (2, 4, 3, 1, 0)).reshape(9, 3, w.shape[1], channels)
        for w in (first, second, third)
    ]
    maps = first_maps(parts, xs, channels)
    maps += spread_maps(xs, channels, True) + spread_maps(xs, channels, False)
    return pl.pallas_call(
        functools.partial(expand_kernel, y_here),
        out_shape=(
            jax.ShapeDtypeStruct((y_here, 3 * full, lanes), BF16),
            jax.ShapeDtypeStruct((2, 3 * full, lanes), BF16),
            jax.ShapeDtypeStruct((2, 9 * WINDOW, WINDOW), BF16),
            jax.ShapeDtypeStruct((2, 9 * WINDOW, xs // 2 * channels), BF16),
        ),
        in_specs=[vmem_spec()] * 12,
        out_specs=(vmem_spec(),) * 4,
        compiler_params=params(),
        cost_estimate=pl.CostEstimate(
            flops=20_000_000_000, bytes_accessed=10_000_000, transcendentals=0
        ),
    )(*by_tap, *maps)


def join(left, right):
    return jnp.concatenate(
        [left[:, :128], left[:, 128:] + right[:, :128], right[:, 128:]], axis=1
    )


def down_one(block):
    rolled = pltpu.roll(block, 1, 0)
    row = lax.broadcasted_iota(jnp.int32, block.shape, 0)
    return jnp.where(row == 0, 0.0, rolled)


def up_one(block):
    count = block.shape[0]
    rolled = pltpu.roll(block, count - 1, 0)
    row = lax.broadcasted_iota(jnp.int32, block.shape, 0)
    return jnp.where(row == count - 1, 0.0, rolled)


def net_kernel(
    place_ref,
    in_ref,
    w1_ref,
    w1_side_ref,
    w2_ref,
    w3_ref,
    b12_ref,
    b3_ref,
    order_ref,
    out_ref,
    spread,
    own,
    before,
    after,
    act1,
    act2,
):
    devices, rows_in, lanes_in = in_ref.shape
    z1, groups = act1.shape[:2]
    z2 = act2.shape[0]
    z_here = z2 - 2
    y_here = groups - 2
    first_z = place_ref[0]
    z_count = place_ref[1]
    window = 256
    lanes = act1.shape[3]

    def taps(act, z, count, h):
        start = h * (lanes - window)
        pieces = []
        for dz in range(3):
            for dy in range(3):
                piece = act[pl.ds(z + dz, count), dy : dy + y_here, :, start : start + window]
                pieces.append(piece.reshape(count * y_here * devices, window))
        return jnp.concatenate(pieces, axis=1)

    @pl.when(pl.program_id(0) == 0)
    def _():
        for s in range(devices):
            piece = in_ref[s].astype(F32)
            for j in range(0, lanes_in, 128):
                spread[j // 128, pl.ds(s, rows_in, stride=devices), :] = piece[:, j : j + 128]

        tiles = [spread.at[j] for j in range(lanes_in // 128)]

        def shift(z, carry):
            base = pl.multiple_of(z * devices, devices)
            block = jnp.concatenate([part[pl.ds(base, devices), :] for part in tiles], axis=1)
            own[pl.ds(base, devices), :] = block.astype(BF16)
            before[pl.ds(base, devices), :] = down_one(block).astype(BF16)
            after[pl.ds(base, devices), :] = up_one(block).astype(BF16)
            return carry

        lax.fori_loop(0, z1 + 2, shift, 0)

        def three(ref):
            count = z1 * devices
            return jnp.concatenate(
                [ref[dz * devices : dz * devices + count, :] for dz in range(3)], axis=1
            )

        for m in range(y_here):
            result = jnp.dot(three(own), w1_ref[m], preferred_element_type=F32)
            if m == 0:
                result += jnp.dot(three(before), w1_side_ref[0], preferred_element_type=F32)
            if m == y_here - 1:
                result += jnp.dot(three(after), w1_side_ref[1], preferred_element_type=F32)
            value = jnp.maximum(result + b12_ref[0:1, :], 0.0).reshape(z1, devices, lanes)
            act1[:, m + 1] = value.astype(BF16)
            for z in range(z1):
                if m == 0:
                    act1[z, groups - 1] = up_one(value[z]).astype(BF16)
                if m == y_here - 1:
                    act1[z, 0] = down_one(value[z]).astype(BF16)
        for z in (0, 1, z1 - 2, z1 - 1):
            here = first_z + z - 2

            @pl.when((here < 0) | (here >= z_count))
            def _():
                act1[z] = jnp.zeros_like(act1[z])

        many = SECOND_GROUP

        def second(step, carry):
            z = step * many
            left = jnp.dot(taps(act1, z, many, 0), w2_ref[0], preferred_element_type=F32)
            right = jnp.dot(taps(act1, z, many, 1), w2_ref[1], preferred_element_type=F32)
            value = jnp.maximum(join(left, right) + b12_ref[1:2, :], 0.0)
            cube = value.reshape(many, y_here, devices, lanes)
            act2[pl.ds(z, many), 1 : groups - 1] = cube.astype(BF16)
            for i in range(many):
                act2[z + i, groups - 1] = up_one(cube[i, 0]).astype(BF16)
                act2[z + i, 0] = down_one(cube[i, y_here - 1]).astype(BF16)
            return carry

        lax.fori_loop(0, z2 // many, second, 0)
        for z in (0, z2 - 1):
            here = first_z + z - 1

            @pl.when((here < 0) | (here >= z_count))
            def _():
                act2[z] = jnp.zeros_like(act2[z])

    channels, many, xs, y_count = out_ref.shape
    z = pl.program_id(0) * many
    parts = []
    for h in range(2):
        result = jnp.dot(taps(act2, z, many, h), w3_ref[h], preferred_element_type=F32)
        value = jnp.maximum(result + b3_ref[...], 0.0).astype(BF16)
        parts.append(value)
    for i in range(many):
        pieces = []
        for value in parts:
            turned = lax.dot_general(
                value[i * y_count : (i + 1) * y_count],
                order_ref[...],
                (((0,), (0,)), ((), ())),
                preferred_element_type=F32,
            )
            pieces.append(turned.reshape(channels, xs // 2, y_count))
        out_ref[:, i] = jnp.concatenate(pieces, axis=1).astype(BF16)


def network(gathered, place, weights, biases, z_here, xs, y_here):
    devices, rows_in, lanes_in = gathered.shape
    channels = biases[0].shape[0]
    y_count = y_here * devices
    lanes = xs * channels
    w1, w1_side, w2, w3 = weights
    b12 = jnp.stack([jnp.tile(biases[0], xs), jnp.tile(biases[1], xs)])
    b3 = jnp.repeat(biases[2], xs // 2)[None]
    row = np.arange(y_count)
    order = np.zeros((y_count, y_count), np.float32)
    order[row, row % devices * y_here + row // devices] = 1.0
    order = jnp.asarray(order, BF16)
    z1, z2 = z_here + 4, z_here + 2
    groups = y_here + 2
    return pl.pallas_call(
        net_kernel,
        out_shape=jax.ShapeDtypeStruct((channels, z_here, xs, y_count), BF16),
        grid=(z_here // THIRD_GROUP,),
        in_specs=[pl.BlockSpec(memory_space=pltpu.SMEM)] + [vmem_spec()] * 8,
        out_specs=pl.BlockSpec((channels, THIRD_GROUP, xs, y_count), lambda z: (0, z, 0, 0)),
        scratch_shapes=[
            pltpu.VMEM((lanes_in // 128, rows_in * devices, 128), F32),
            pltpu.VMEM((rows_in * devices, lanes_in), BF16),
            pltpu.VMEM((rows_in * devices, lanes_in), BF16),
            pltpu.VMEM((rows_in * devices, lanes_in), BF16),
            pltpu.VMEM((z1, groups, devices, lanes), BF16),
            pltpu.VMEM((z2, groups, devices, lanes), BF16),
        ],
        compiler_params=params(),
    )(place, gathered, w1, w1_side, w2, w3, b12, b3, order)


def on_device(
    kspace,
    sensitivity,
    weight_first,
    bias_first,
    weight_second,
    bias_second,
    weight_third,
    bias_third,
):
    devices = lax.axis_size("kz")
    _, y_here, _, xs, z_count = sensitivity.shape
    z_here = z_count // devices
    lines = y_transform(kspace, devices)
    received = lax.all_to_all(lines, "kz", 0, 0)
    weights = expand_weights(weight_first, weight_second, weight_third, y_here, xs)
    received, weights = lax.optimization_barrier((received, weights))
    merged = z_transform(received, sensitivity, devices)
    gathered = lax.all_to_all(merged, "kz", 0, 0)
    place = jnp.stack([lax.axis_index("kz") * z_here, z_count]).astype(jnp.int32)
    biases = (bias_first, bias_second, bias_third)
    return network(gathered, place, weights, biases, z_here, xs, y_here)


def solution(mesh):
    in_specs = (
        P("grp", None, "kz", None),
        P(None, ("grp", "kz"), None, None, None),
        P(),
        P(),
        P(),
        P(),
        P(),
        P(),
    )
    out_specs = P("grp", "kz", None, None)
    return jax.shard_map(
        on_device, mesh=mesh, in_specs=in_specs, out_specs=out_specs, check_vma=False
    )
```

```python
import functools
import math

import jax
import jax.numpy as jnp
import numpy as np
from jax import lax
from jax.experimental import pallas as pl
from jax.experimental.pallas import tpu as pltpu
from jax.sharding import PartitionSpec as P

BF16 = jnp.bfloat16
F32 = jnp.float32
HALO = 3
WINDOW = 256
Y_GROUP = 4
Y_PASSES = 3
Z_WIDTH = 128
CODE_SCALE = 2.0**20
SECOND_GROUP = 3
THIRD_GROUP = 4
VMEM_LIMIT = 56 * 1024 * 1024


def round_up(value, unit):
    return -(-value // unit) * unit


def params():
    return pltpu.CompilerParams(vmem_limit_bytes=VMEM_LIMIT)


def vmem_spec():
    return pl.BlockSpec(memory_space=pltpu.VMEM)


def halves(table):
    high = table.astype(jnp.bfloat16)
    low = (table - high.astype(np.float64)).astype(jnp.bfloat16)
    return high, low


def trig(length, rows, cols):
    phase = (rows[:, None] * cols[None, :]) % length
    angle = phase * (2.0 * math.pi / length)
    return np.cos(angle), np.sin(angle)


def parities(kz_here):
    return 2 if kz_here % 16 == 0 else 1


def y_table(y_count, devices):
    y_here = y_count // devices
    order = (np.arange(devices)[None, :] * y_here + np.arange(y_here)[:, None]).reshape(-1)
    cosine, sine = trig(y_count, order, np.arange(y_count))
    real = np.concatenate([cosine, -sine], axis=1)
    imag = np.concatenate([sine, cosine], axis=1)
    return np.concatenate([real, imag], axis=0) * (CODE_SCALE / math.sqrt(y_count))


def z_table(z_count, devices, groups, width):
    kz_here = z_count // devices
    outputs = z_count // groups
    tables = []
    for parity in range(groups):
        kz = np.arange(devices)[:, None] * kz_here + np.arange(parity, kz_here, groups)[None, :]
        cosine, sine = trig(z_count, kz.reshape(-1), np.arange(outputs))
        both = np.stack([np.stack([cosine, sine], 1), np.stack([-sine, cosine], 1)], 0)
        both = both.reshape(2, devices, kz_here // groups, 2, outputs // width, width)
        both = both.transpose(4, 1, 0, 2, 3, 5)
        tables.append(both.reshape(outputs // width, 2 * z_count // groups, 2 * width))
    return np.stack(tables)


def encode(value):
    square = value * jnp.abs(value)
    return (square * jnp.abs(square)).astype(BF16)


def decode(code):
    code = code.astype(F32)
    size = jnp.maximum(jnp.abs(code), 1e-37)
    inverse = lax.rsqrt(size * lax.rsqrt(size))
    return code * (inverse * inverse * inverse)


def y_kernel(devices, k_ref, t_ref, out_ref, lines, turned, sems):
    kz_here, pairs, _ = lines.shape
    rows = t_ref.shape[0]
    group = min(Y_GROUP, kz_here)
    groups = parities(kz_here)

    def fetch(kz):
        return pltpu.make_async_copy(k_ref.at[:, kz, :], lines.at[kz], sems.at[kz])

    for kz in range(kz_here):
        fetch(kz).start()
    for first in range(0, kz_here, group):
        for kz in range(first, first + group):
            fetch(kz).wait()
        line = lines[first : first + group].reshape(group * pairs, lines.shape[2])
        high = line.astype(BF16)
        terms = [high]
        if Y_PASSES > 1:
            terms.append(high)
        if Y_PASSES > 2:
            terms.append((line - high.astype(F32)).astype(BF16))
        operand = jnp.concatenate(terms, axis=1)
        result = lax.dot_general(
            t_ref[...], operand, (((1,), (1,)), ((), ())), preferred_element_type=F32
        )
        block = 2 * kz_here
        half = rows // 2
        for i in range(group):
            kz = first + i
            for part in range(2):
                place = kz % groups * (block // groups)
                place += part * (kz_here // groups) + kz // groups
                turned[pl.ds(place, half, stride=block), :] = result[
                    part * half : (part + 1) * half, i * pairs : (i + 1) * pairs
                ]
    for row in range(rows // 2):
        y, device = row // devices, row % devices
        out_ref[device, :, y * pairs : (y + 1) * pairs] = encode(
            turned[row * block : (row + 1) * block, :]
        )


def y_transform(kspace, devices):
    coils, xs, kz_here, width = kspace.shape
    pairs = coils * xs
    y_count = width // 2
    high, low = halves(y_table(y_count, devices))
    table = jnp.asarray(np.concatenate([high, low, high][:Y_PASSES], axis=1))
    return pl.pallas_call(
        functools.partial(y_kernel, devices),
        out_shape=jax.ShapeDtypeStruct((devices, 2 * kz_here, y_count // devices * pairs), BF16),
        in_specs=[pl.BlockSpec(memory_space=pl.ANY), vmem_spec()],
        out_specs=vmem_spec(),
        scratch_shapes=[
            pltpu.VMEM((kz_here, pairs, width), F32),
            pltpu.VMEM((2 * y_count * kz_here, pairs), F32),
            pltpu.SemaphoreType.DMA((kz_here,)),
        ],
        compiler_params=params(),
    )(kspace.reshape(pairs, kz_here, width), table)


def z_kernel(scale, devices, z_here, groups, r_ref, t_ref, *refs):
    s_refs, out_ref, codes, lines, turned = refs[:groups], *refs[groups:]
    step = pl.program_id(0)
    _, y_here, coils, xs, width = s_refs[0].shape
    lanes = out_ref.shape[2]
    columns = r_ref.shape[2]
    rows = r_ref.shape[1] // groups
    depth = devices * rows

    @pl.when(step == 0)
    def _():
        for parity in range(groups):
            piece = r_ref[:, parity * rows : (parity + 1) * rows, :]
            codes[parity] = piece.reshape(depth, columns).T
        turned[...] = jnp.zeros_like(turned)

        def unpack(i, carry):
            at = pl.ds(pl.multiple_of(i * 64, 64), 64)
            for parity in range(groups):
                value = decode(codes[parity, at, :])
                high = value.astype(BF16)
                lines[parity, at, :depth] = high
                lines[parity, at, depth:] = (value - high.astype(F32)).astype(BF16)
            return carry

        lax.fori_loop(0, columns // 64, unpack, 0)

    products = []
    for parity in range(groups):
        operand = lines[parity]
        operand = jnp.concatenate([operand, operand[:, :depth]], axis=1)
        products.append(jnp.dot(operand, t_ref[parity, 0], preferred_element_type=F32))
    if groups == 2:
        products = [products[0] + products[1], products[0] - products[1]]
    for part, (images, s_ref) in enumerate(zip(products, s_refs)):
        image_re = images[:, :width].reshape(y_here, coils, xs, width)
        image_im = images[:, width:].reshape(y_here, coils, xs, width)
        sens_re = s_ref[0]
        sens_im = s_ref[1]
        real = jnp.sum(sens_re * image_re + sens_im * image_im, axis=1) * scale
        imag = jnp.sum(sens_re * image_im - sens_im * image_re, axis=1) * scale
        merged = jnp.concatenate([real, imag], axis=1).reshape(y_here * 2 * xs, width)
        extra = lanes - y_here * 2 * xs
        if extra:
            merged = jnp.concatenate([merged, jnp.zeros((extra, width), F32)], axis=0)
        base = 8 + part * devices * z_here // groups
        base = pl.multiple_of(base + step * width, 8)
        turned[pl.ds(base, width), :] = merged.T

    @pl.when(step == pl.num_programs(0) - 1)
    def _():
        for device in range(devices):
            first = 8 + device * z_here - HALO
            out_ref[device] = turned[first : first + out_ref.shape[1], :].astype(BF16)


def z_transform(received, sensitivity, devices):
    _, y_here, coils, xs, z_count = sensitivity.shape
    pairs = coils * xs
    width = Z_WIDTH
    groups = parities(z_count // devices)
    high, low = halves(z_table(z_count, devices, groups, width))
    table = jnp.asarray(np.concatenate([high, high, low], axis=2))
    scale = 1.0 / (math.sqrt(z_count) * CODE_SCALE)
    rows = round_up(z_count // devices + 2 * HALO, 8)
    lanes = round_up(y_here * 2 * xs, 128)
    steps = z_count // groups // width
    depth = 2 * z_count // groups

    def sens_spec(part):
        return pl.BlockSpec(
            (2, y_here, coils, xs, width), lambda z: (0, 0, 0, 0, z + part * steps)
        )

    return pl.pallas_call(
        functools.partial(z_kernel, scale, devices, z_count // devices, groups),
        out_shape=jax.ShapeDtypeStruct((devices, rows, lanes), BF16),
        grid=(steps,),
        in_specs=[
            pl.BlockSpec(received.shape, lambda z: (0, 0, 0)),
            pl.BlockSpec((groups, 1, 3 * depth, 2 * width), lambda z: (0, z, 0, 0)),
        ]
        + [sens_spec(part) for part in range(groups)],
        out_specs=pl.BlockSpec((devices, rows, lanes), lambda z: (0, 0, 0)),
        scratch_shapes=[
            pltpu.VMEM((groups, y_here * pairs, depth), BF16),
            pltpu.VMEM((groups, y_here * pairs, 2 * depth), BF16),
            pltpu.VMEM((8 + z_count + 32, lanes), F32),
        ],
        compiler_params=params(),
    )(received, table, *[sensitivity] * groups)


def window_starts(lanes):
    return (0, lanes - WINDOW)


def column_map(xs, channels, x_major):
    half = xs // 2
    found = []
    for h in range(2):
        x, c = np.meshgrid(np.arange(half) + h * half, np.arange(channels), indexing="ij")
        if x_major:
            pad = np.full(WINDOW - half * channels, -9)
            x, c = x.reshape(-1), c.reshape(-1)
            order = [(pad, x), (pad, c)] if h else [(x, pad), (c, pad)]
            found.append((np.concatenate(order[0]), np.concatenate(order[1])))
        else:
            found.append((x.T.reshape(-1), c.T.reshape(-1)))
    return found


def band_masks(x_in, x_out):
    taps = np.arange(3)[:, None, None]
    return (x_in[None, :, None] == x_out[None, None, :] + taps - 1).astype(np.float32)


def spread_maps(xs, channels, x_major):
    rows_of, columns_of, masks = [], [], []
    lanes = xs * channels
    for start, (x_out, c_out) in zip(window_starts(lanes), column_map(xs, channels, x_major)):
        lane = start + np.arange(WINDOW)
        rows_of.append(lane[:, None] % channels == np.arange(channels)[None, :])
        columns_of.append(np.arange(channels)[:, None] == c_out[None, :])
        masks.append(band_masks(lane // channels, x_out))
    return [jnp.asarray(np.stack(m).astype(np.float32), BF16) for m in (rows_of, columns_of, masks)]


def first_maps(parts, xs, channels):
    row = np.arange(parts * xs)
    lane = np.arange(xs * channels)
    rows_of = row[:, None] // xs == np.arange(parts)[None, :]
    columns_of = np.arange(channels)[:, None] == lane[None, :] % channels
    masks = band_masks(row % xs, lane // channels)
    return [jnp.asarray(np.asarray(m, np.float32), BF16) for m in (rows_of, columns_of, masks)]


def spread_tap(kernel_ref, tap, rows_of, columns_of, masks):
    total = None
    for dx in range(3):
        tall = jnp.dot(rows_of, kernel_ref[tap, dx], preferred_element_type=F32).astype(BF16)
        wide = jnp.dot(tall, columns_of, preferred_element_type=F32)
        term = wide * masks[dx].astype(F32)
        total = term if total is None else total + term
    return total.astype(BF16)


def expand_kernel(
    y_here,
    k1_ref,
    k2_ref,
    k3_ref,
    r1_ref,
    c1_ref,
    m1_ref,
    r2_ref,
    c2_ref,
    m2_ref,
    r3_ref,
    c3_ref,
    m3_ref,
    w1_ref,
    side_ref,
    w2_ref,
    w3_ref,
):
    piece = r1_ref.shape[0]
    full = w1_ref.shape[1] // 3
    w1_ref[...] = jnp.zeros_like(w1_ref)
    side_ref[...] = jnp.zeros_like(side_ref)
    for dz in range(3):
        for dy in range(3):
            tap = dz * 3 + dy
            block = spread_tap(k1_ref, tap, r1_ref[...], c1_ref[...], m1_ref)
            for m in range(y_here):
                y = m + dy - 1
                if 0 <= y < y_here:
                    base = dz * full + y * piece
                    w1_ref[m, base : base + piece, :] = block
            if dy == 0:
                base = dz * full + (y_here - 1) * piece
                side_ref[0, base : base + piece, :] = block
            if dy == 2:
                side_ref[1, dz * full : dz * full + piece, :] = block

    def deep(tap, carry):
        base = pl.multiple_of(tap * WINDOW, WINDOW)
        for h in range(2):
            w2_ref[h, pl.ds(base, WINDOW), :] = spread_tap(
                k2_ref, tap, r2_ref[h], c2_ref[h], m2_ref.at[h]
            )
            w3_ref[h, pl.ds(base, WINDOW), :] = spread_tap(
                k3_ref, tap, r3_ref[h], c3_ref[h], m3_ref.at[h]
            )
        return carry

    lax.fori_loop(0, 9, deep, 0)


def expand_weights(first, second, third, y_here, xs):
    channels, parts = first.shape[:2]
    full = round_up(y_here * parts * xs, 128)
    lanes = xs * channels
    by_tap = [
        jnp.transpose(w, (2, 4, 3, 1, 0)).reshape(9, 3, w.shape[1], channels)
        for w in (first, second, third)
    ]
    maps = first_maps(parts, xs, channels)
    maps += spread_maps(xs, channels, True) + spread_maps(xs, channels, False)
    return pl.pallas_call(
        functools.partial(expand_kernel, y_here),
        out_shape=(
            jax.ShapeDtypeStruct((y_here, 3 * full, lanes), BF16),
            jax.ShapeDtypeStruct((2, 3 * full, lanes), BF16),
            jax.ShapeDtypeStruct((2, 9 * WINDOW, WINDOW), BF16),
            jax.ShapeDtypeStruct((2, 9 * WINDOW, xs // 2 * channels), BF16),
        ),
        in_specs=[vmem_spec()] * 12,
        out_specs=(vmem_spec(),) * 4,
        compiler_params=params(),
        cost_estimate=pl.CostEstimate(
            flops=20_000_000_000, bytes_accessed=10_000_000, transcendentals=0
        ),
    )(*by_tap, *maps)


def join(left, right):
    return jnp.concatenate(
        [left[:, :128], left[:, 128:] + right[:, :128], right[:, 128:]], axis=1
    )


def down_one(block):
    rolled = pltpu.roll(block, 1, 0)
    row = lax.broadcasted_iota(jnp.int32, block.shape, 0)
    return jnp.where(row == 0, 0.0, rolled)


def up_one(block):
    count = block.shape[0]
    rolled = pltpu.roll(block, count - 1, 0)
    row = lax.broadcasted_iota(jnp.int32, block.shape, 0)
    return jnp.where(row == count - 1, 0.0, rolled)


def net_kernel(
    place_ref,
    in_ref,
    w1_far,
    w1_side_far,
    w2_far,
    w3_far,
    b12_ref,
    b3_ref,
    order_ref,
    out_ref,
    spread,
    own,
    before,
    after,
    act1,
    act2,
    w1_ref,
    w1_side_ref,
    w2_ref,
    w3_ref,
    sems,
):
    devices, rows_in, lanes_in = in_ref.shape
    z1, groups = act1.shape[:2]
    z2 = act2.shape[0]
    z_here = z2 - 2
    y_here = groups - 2
    first_z = place_ref[0]
    z_count = place_ref[1]
    window = 256
    lanes = act1.shape[3]

    def taps(act, z, count, h):
        start = h * (lanes - window)
        pieces = []
        for dz in range(3):
            for dy in range(3):
                piece = act[pl.ds(z + dz, count), dy : dy + y_here, :, start : start + window]
                pieces.append(piece.reshape(count * y_here * devices, window))
        return jnp.concatenate(pieces, axis=1)

    first_copies = [
        pltpu.make_async_copy(w1_far.at[m], w1_ref.at[m], sems.at[m]) for m in range(y_here)
    ]
    side_copy = pltpu.make_async_copy(w1_side_far, w1_side_ref, sems.at[y_here])
    second_copy = pltpu.make_async_copy(w2_far, w2_ref, sems.at[y_here + 1])
    third_copy = pltpu.make_async_copy(w3_far, w3_ref, sems.at[y_here + 2])

    @pl.when(pl.program_id(0) == 0)
    def _():
        side_copy.start()
        for copy in first_copies:
            copy.start()
        second_copy.start()
        third_copy.start()
        for s in range(devices):
            piece = in_ref[s].astype(F32)
            for j in range(0, lanes_in, 128):
                spread[j // 128, pl.ds(s, rows_in, stride=devices), :] = piece[:, j : j + 128]

        tiles = [spread.at[j] for j in range(lanes_in // 128)]

        def shift(z, carry):
            base = pl.multiple_of(z * devices, devices)
            block = jnp.concatenate([part[pl.ds(base, devices), :] for part in tiles], axis=1)
            own[pl.ds(base, devices), :] = block.astype(BF16)
            before[pl.ds(base, devices), :] = down_one(block).astype(BF16)
            after[pl.ds(base, devices), :] = up_one(block).astype(BF16)
            return carry

        lax.fori_loop(0, z1 + 2, shift, 0)

        def three(ref):
            count = z1 * devices
            return jnp.concatenate(
                [ref[dz * devices : dz * devices + count, :] for dz in range(3)], axis=1
            )

        side_copy.wait()
        for m in range(y_here):
            first_copies[m].wait()
            result = jnp.dot(three(own), w1_ref[m], preferred_element_type=F32)
            if m == 0:
                result += jnp.dot(three(before), w1_side_ref[0], preferred_element_type=F32)
            if m == y_here - 1:
                result += jnp.dot(three(after), w1_side_ref[1], preferred_element_type=F32)
            value = jnp.maximum(result + b12_ref[0:1, :], 0.0).reshape(z1, devices, lanes)
            act1[:, m + 1] = value.astype(BF16)
            for z in range(z1):
                if m == 0:
                    act1[z, groups - 1] = up_one(value[z]).astype(BF16)
                if m == y_here - 1:
                    act1[z, 0] = down_one(value[z]).astype(BF16)
        for z in (0, 1, z1 - 2, z1 - 1):
            here = first_z + z - 2

            @pl.when((here < 0) | (here >= z_count))
            def _():
                act1[z] = jnp.zeros_like(act1[z])

        many = SECOND_GROUP

        def second(step, carry):
            z = step * many
            left = jnp.dot(taps(act1, z, many, 0), w2_ref[0], preferred_element_type=F32)
            right = jnp.dot(taps(act1, z, many, 1), w2_ref[1], preferred_element_type=F32)
            value = jnp.maximum(join(left, right) + b12_ref[1:2, :], 0.0)
            cube = value.reshape(many, y_here, devices, lanes)
            act2[pl.ds(z, many), 1 : groups - 1] = cube.astype(BF16)
            for i in range(many):
                act2[z + i, groups - 1] = up_one(cube[i, 0]).astype(BF16)
                act2[z + i, 0] = down_one(cube[i, y_here - 1]).astype(BF16)
            return carry

        second_copy.wait()
        lax.fori_loop(0, z2 // many, second, 0)
        third_copy.wait()
        for z in (0, z2 - 1):
            here = first_z + z - 1

            @pl.when((here < 0) | (here >= z_count))
            def _():
                act2[z] = jnp.zeros_like(act2[z])

    channels, many, xs, y_count = out_ref.shape
    z = pl.program_id(0) * many
    parts = []
    for h in range(2):
        result = jnp.dot(taps(act2, z, many, h), w3_ref[h], preferred_element_type=F32)
        value = jnp.maximum(result + b3_ref[...], 0.0).astype(BF16)
        parts.append(value)
    for i in range(many):
        pieces = []
        for value in parts:
            turned = lax.dot_general(
                value[i * y_count : (i + 1) * y_count],
                order_ref[...],
                (((0,), (0,)), ((), ())),
                preferred_element_type=F32,
            )
            pieces.append(turned.reshape(channels, xs // 2, y_count))
        out_ref[:, i] = jnp.concatenate(pieces, axis=1).astype(BF16)


def network(gathered, place, weights, biases, z_here, xs, y_here):
    devices, rows_in, lanes_in = gathered.shape
    channels = biases[0].shape[0]
    y_count = y_here * devices
    lanes = xs * channels
    w1, w1_side, w2, w3 = weights
    b12 = jnp.stack([jnp.tile(biases[0], xs), jnp.tile(biases[1], xs)])
    b3 = jnp.repeat(biases[2], xs // 2)[None]
    row = np.arange(y_count)
    order = np.zeros((y_count, y_count), np.float32)
    order[row, row % devices * y_here + row // devices] = 1.0
    order = jnp.asarray(order, BF16)
    z1, z2 = z_here + 4, z_here + 2
    groups = y_here + 2
    return pl.pallas_call(
        net_kernel,
        out_shape=jax.ShapeDtypeStruct((channels, z_here, xs, y_count), BF16),
        grid=(z_here // THIRD_GROUP,),
        in_specs=[pl.BlockSpec(memory_space=pltpu.SMEM), vmem_spec()]
        + [pl.BlockSpec(memory_space=pl.ANY)] * 4
        + [vmem_spec()] * 3,
        out_specs=pl.BlockSpec((channels, THIRD_GROUP, xs, y_count), lambda z: (0, z, 0, 0)),
        scratch_shapes=[
            pltpu.VMEM((lanes_in // 128, rows_in * devices, 128), F32),
            pltpu.VMEM((rows_in * devices, lanes_in), BF16),
            pltpu.VMEM((rows_in * devices, lanes_in), BF16),
            pltpu.VMEM((rows_in * devices, lanes_in), BF16),
            pltpu.VMEM((z1, groups, devices, lanes), BF16),
            pltpu.VMEM((z2, groups, devices, lanes), BF16),
            pltpu.VMEM(w1.shape, BF16),
            pltpu.VMEM(w1_side.shape, BF16),
            pltpu.VMEM(w2.shape, BF16),
            pltpu.VMEM(w3.shape, BF16),
            pltpu.SemaphoreType.DMA((y_here + 3,)),
        ],
        compiler_params=params(),
    )(place, gathered, w1, w1_side, w2, w3, b12, b3, order)


def on_device(
    kspace,
    sensitivity,
    weight_first,
    bias_first,
    weight_second,
    bias_second,
    weight_third,
    bias_third,
):
    devices = lax.axis_size("kz")
    _, y_here, _, xs, z_count = sensitivity.shape
    z_here = z_count // devices
    lines = y_transform(kspace, devices)
    received = lax.all_to_all(lines, "kz", 0, 0)
    weights = expand_weights(weight_first, weight_second, weight_third, y_here, xs)
    received, weights = lax.optimization_barrier((received, weights))
    merged = z_transform(received, sensitivity, devices)
    gathered = lax.all_to_all(merged, "kz", 0, 0)
    place = jnp.stack([lax.axis_index("kz") * z_here, z_count]).astype(jnp.int32)
    biases = (bias_first, bias_second, bias_third)
    return network(gathered, place, weights, biases, z_here, xs, y_here)


def solution(mesh):
    in_specs = (
        P("grp", None, "kz", None),
        P(None, ("grp", "kz"), None, None, None),
        P(),
        P(),
        P(),
        P(),
        P(),
        P(),
    )
    out_specs = P("grp", "kz", None, None)
    return jax.shard_map(
        on_device, mesh=mesh, in_specs=in_specs, out_specs=out_specs, check_vma=False
    )
```

```python
import functools
import math

import jax
import jax.numpy as jnp
import numpy as np
from jax import lax
from jax.experimental import pallas as pl
from jax.experimental.pallas import tpu as pltpu
from jax.sharding import PartitionSpec as P

BF16 = jnp.bfloat16
F32 = jnp.float32
HALO = 3
WINDOW = 256
Y_GROUP = 4
Y_PASSES = 3
Z_WIDTH = 128
CODE_SCALE = 2.0**20
SECOND_GROUP = 6
THIRD_GROUP = 8
VMEM_LIMIT = 56 * 1024 * 1024


def round_up(value, unit):
    return -(-value // unit) * unit


def params():
    return pltpu.CompilerParams(vmem_limit_bytes=VMEM_LIMIT)


def vmem_spec():
    return pl.BlockSpec(memory_space=pltpu.VMEM)


def halves(table):
    high = table.astype(jnp.bfloat16)
    low = (table - high.astype(np.float64)).astype(jnp.bfloat16)
    return high, low


def trig(length, rows, cols):
    phase = (rows[:, None] * cols[None, :]) % length
    angle = phase * (2.0 * math.pi / length)
    return np.cos(angle), np.sin(angle)


def parities(kz_here):
    return 2 if kz_here % 16 == 0 else 1


def y_table(y_count, devices):
    y_here = y_count // devices
    order = (np.arange(devices)[None, :] * y_here + np.arange(y_here)[:, None]).reshape(-1)
    cosine, sine = trig(y_count, order, np.arange(y_count))
    real = np.concatenate([cosine, -sine], axis=1)
    imag = np.concatenate([sine, cosine], axis=1)
    return np.concatenate([real, imag], axis=0) * (CODE_SCALE / math.sqrt(y_count))


def z_table(z_count, devices, groups, width):
    kz_here = z_count // devices
    outputs = z_count // groups
    tables = []
    for parity in range(groups):
        kz = np.arange(devices)[:, None] * kz_here + np.arange(parity, kz_here, groups)[None, :]
        cosine, sine = trig(z_count, kz.reshape(-1), np.arange(outputs))
        both = np.stack([np.stack([cosine, sine], 1), np.stack([-sine, cosine], 1)], 0)
        both = both.reshape(2, devices, kz_here // groups, 2, outputs // width, width)
        both = both.transpose(4, 1, 0, 2, 3, 5)
        tables.append(both.reshape(outputs // width, 2 * z_count // groups, 2 * width))
    return np.stack(tables)


def encode(value):
    square = value * jnp.abs(value)
    return (square * jnp.abs(square)).astype(BF16)


def decode(code):
    code = code.astype(F32)
    size = jnp.maximum(jnp.abs(code), 1e-37)
    inverse = lax.rsqrt(size * lax.rsqrt(size))
    return code * (inverse * inverse * inverse)


def y_kernel(devices, k_ref, t_ref, out_ref, lines, turned, sems):
    kz_here, pairs, _ = lines.shape
    rows = t_ref.shape[0]
    group = min(Y_GROUP, kz_here)
    groups = parities(kz_here)

    def fetch(kz):
        return pltpu.make_async_copy(k_ref.at[:, kz, :], lines.at[kz], sems.at[kz])

    for kz in range(kz_here):
        fetch(kz).start()
    for first in range(0, kz_here, group):
        for kz in range(first, first + group):
            fetch(kz).wait()
        line = lines[first : first + group].reshape(group * pairs, lines.shape[2])
        high = line.astype(BF16)
        terms = [high]
        if Y_PASSES > 1:
            terms.append(high)
        if Y_PASSES > 2:
            terms.append((line - high.astype(F32)).astype(BF16))
        operand = jnp.concatenate(terms, axis=1)
        result = lax.dot_general(
            t_ref[...], operand, (((1,), (1,)), ((), ())), preferred_element_type=F32
        )
        block = 2 * kz_here
        half = rows // 2
        for i in range(group):
            kz = first + i
            for part in range(2):
                place = kz % groups * (block // groups)
                place += part * (kz_here // groups) + kz // groups
                turned[pl.ds(place, half, stride=block), :] = result[
                    part * half : (part + 1) * half, i * pairs : (i + 1) * pairs
                ]
    for row in range(rows // 2):
        y, device = row // devices, row % devices
        out_ref[device, :, y * pairs : (y + 1) * pairs] = encode(
            turned[row * block : (row + 1) * block, :]
        )


def y_transform(kspace, devices):
    coils, xs, kz_here, width = kspace.shape
    pairs = coils * xs
    y_count = width // 2
    high, low = halves(y_table(y_count, devices))
    table = jnp.asarray(np.concatenate([high, low, high][:Y_PASSES], axis=1))
    return pl.pallas_call(
        functools.partial(y_kernel, devices),
        out_shape=jax.ShapeDtypeStruct((devices, 2 * kz_here, y_count // devices * pairs), BF16),
        in_specs=[pl.BlockSpec(memory_space=pl.ANY), vmem_spec()],
        out_specs=vmem_spec(),
        scratch_shapes=[
            pltpu.VMEM((kz_here, pairs, width), F32),
            pltpu.VMEM((2 * y_count * kz_here, pairs), F32),
            pltpu.SemaphoreType.DMA((kz_here,)),
        ],
        compiler_params=params(),
    )(kspace.reshape(pairs, kz_here, width), table)


def z_kernel(
    scale, z_here, groups, r_ref, t_far, s_far, out_ref, codes, lines, turned, t_ref, s_ref, sems
):
    devices = r_ref.shape[0]
    steps, _, _, y_here, coils, xs, width = s_ref.shape
    lanes = out_ref.shape[2]
    columns = r_ref.shape[2]
    rows = r_ref.shape[1] // groups
    depth = devices * rows
    copies = []
    for step in range(steps):
        found = [
            pltpu.make_async_copy(
                t_far.at[:, step], t_ref.at[:, step], sems.at[step * (groups + 1) + groups]
            )
        ]
        for part in range(groups):
            z = pl.ds((part * steps + step) * width, width)
            found.append(
                pltpu.make_async_copy(
                    s_far.at[:, :, :, :, z],
                    s_ref.at[step, part],
                    sems.at[step * (groups + 1) + part],
                )
            )
        copies.append(found)
    for found in copies:
        for copy in found:
            copy.start()
    for parity in range(groups):
        piece = r_ref[:, parity * rows : (parity + 1) * rows, :]
        codes[parity] = piece.reshape(depth, columns).T
    turned[...] = jnp.zeros_like(turned)

    def unpack(i, carry):
        at = pl.ds(pl.multiple_of(i * 64, 64), 64)
        for parity in range(groups):
            value = decode(codes[parity, at, :])
            high = value.astype(BF16)
            lines[parity, at, :depth] = high
            lines[parity, at, depth:] = (value - high.astype(F32)).astype(BF16)
        return carry

    lax.fori_loop(0, columns // 64, unpack, 0)
    for step in range(steps):
        for copy in copies[step]:
            copy.wait()
        z_step(scale, groups, step, lines, t_ref, s_ref, turned)
    for device in range(devices):
        first = 8 + device * z_here - HALO
        out_ref[device] = turned[first : first + out_ref.shape[1], :].astype(BF16)


def z_step(scale, groups, step, lines, t_ref, s_ref, turned):
    steps, _, _, y_here, coils, xs, width = s_ref.shape
    depth = lines.shape[2] // 2
    lanes = turned.shape[1]
    products = []
    for parity in range(groups):
        operand = lines[parity]
        operand = jnp.concatenate([operand, operand[:, :depth]], axis=1)
        products.append(jnp.dot(operand, t_ref[parity, step], preferred_element_type=F32))
    if groups == 2:
        products = [products[0] + products[1], products[0] - products[1]]
    for part, images in enumerate(products):
        image_re = images[:, :width].reshape(y_here, coils, xs, width)
        image_im = images[:, width:].reshape(y_here, coils, xs, width)
        sens_re = s_ref[step, part, 0]
        sens_im = s_ref[step, part, 1]
        real = jnp.sum(sens_re * image_re + sens_im * image_im, axis=1) * scale
        imag = jnp.sum(sens_re * image_im - sens_im * image_re, axis=1) * scale
        merged = jnp.concatenate([real, imag], axis=1).reshape(y_here * 2 * xs, width)
        extra = lanes - y_here * 2 * xs
        if extra:
            merged = jnp.concatenate([merged, jnp.zeros((extra, width), F32)], axis=0)
        base = 8 + (part * steps + step) * width
        turned[base : base + width, :] = merged.T


def z_transform(received, sensitivity, devices):
    _, y_here, coils, xs, z_count = sensitivity.shape
    pairs = coils * xs
    width = Z_WIDTH
    groups = parities(z_count // devices)
    high, low = halves(z_table(z_count, devices, groups, width))
    table = jnp.asarray(np.concatenate([high, high, low], axis=2))
    scale = 1.0 / (math.sqrt(z_count) * CODE_SCALE)
    rows = round_up(z_count // devices + 2 * HALO, 8)
    lanes = round_up(y_here * 2 * xs, 128)
    steps = z_count // groups // width
    depth = 2 * z_count // groups

    return pl.pallas_call(
        functools.partial(z_kernel, scale, z_count // devices, groups),
        out_shape=jax.ShapeDtypeStruct((devices, rows, lanes), BF16),
        in_specs=[vmem_spec()] + [pl.BlockSpec(memory_space=pl.ANY)] * 2,
        out_specs=vmem_spec(),
        scratch_shapes=[
            pltpu.VMEM((groups, y_here * pairs, depth), BF16),
            pltpu.VMEM((groups, y_here * pairs, 2 * depth), BF16),
            pltpu.VMEM((8 + z_count + 32, lanes), F32),
            pltpu.VMEM(table.shape, BF16),
            pltpu.VMEM((steps, groups, 2, y_here, coils, xs, width), F32),
            pltpu.SemaphoreType.DMA((steps * (groups + 1),)),
        ],
        compiler_params=params(),
    )(received, table, sensitivity)


def window_starts(lanes):
    return (0, lanes - WINDOW)


def column_map(xs, channels, x_major):
    half = xs // 2
    found = []
    for h in range(2):
        x, c = np.meshgrid(np.arange(half) + h * half, np.arange(channels), indexing="ij")
        if x_major:
            pad = np.full(WINDOW - half * channels, -9)
            x, c = x.reshape(-1), c.reshape(-1)
            order = [(pad, x), (pad, c)] if h else [(x, pad), (c, pad)]
            found.append((np.concatenate(order[0]), np.concatenate(order[1])))
        else:
            found.append((x.T.reshape(-1), c.T.reshape(-1)))
    return found


def band_masks(x_in, x_out):
    taps = np.arange(3)[:, None, None]
    return (x_in[None, :, None] == x_out[None, None, :] + taps - 1).astype(np.float32)


def spread_maps(xs, channels, x_major):
    rows_of, columns_of, masks = [], [], []
    lanes = xs * channels
    for start, (x_out, c_out) in zip(window_starts(lanes), column_map(xs, channels, x_major)):
        lane = start + np.arange(WINDOW)
        rows_of.append(lane[:, None] % channels == np.arange(channels)[None, :])
        columns_of.append(np.arange(channels)[:, None] == c_out[None, :])
        masks.append(band_masks(lane // channels, x_out))
    return [jnp.asarray(np.stack(m).astype(np.float32), BF16) for m in (rows_of, columns_of, masks)]


def first_maps(parts, xs, channels):
    row = np.arange(parts * xs)
    lane = np.arange(xs * channels)
    rows_of = row[:, None] // xs == np.arange(parts)[None, :]
    columns_of = np.arange(channels)[:, None] == lane[None, :] % channels
    masks = band_masks(row % xs, lane // channels)
    return [jnp.asarray(np.asarray(m, np.float32), BF16) for m in (rows_of, columns_of, masks)]


def spread_tap(kernel_ref, tap, rows_of, columns_of, masks):
    total = None
    for dx in range(3):
        tall = jnp.dot(rows_of, kernel_ref[tap, dx], preferred_element_type=F32).astype(BF16)
        wide = jnp.dot(tall, columns_of, preferred_element_type=F32)
        term = wide * masks[dx].astype(F32)
        total = term if total is None else total + term
    return total.astype(BF16)


def expand_kernel(
    y_here,
    k1_ref,
    k2_ref,
    k3_ref,
    r1_ref,
    c1_ref,
    m1_ref,
    r2_ref,
    c2_ref,
    m2_ref,
    r3_ref,
    c3_ref,
    m3_ref,
    w1_ref,
    side_ref,
    w2_ref,
    w3_ref,
):
    piece = r1_ref.shape[0]
    full = w1_ref.shape[1] // 3
    w1_ref[...] = jnp.zeros_like(w1_ref)
    side_ref[...] = jnp.zeros_like(side_ref)
    for dz in range(3):
        for dy in range(3):
            tap = dz * 3 + dy
            block = spread_tap(k1_ref, tap, r1_ref[...], c1_ref[...], m1_ref)
            for m in range(y_here):
                y = m + dy - 1
                if 0 <= y < y_here:
                    base = dz * full + y * piece
                    w1_ref[m, base : base + piece, :] = block
            if dy == 0:
                base = dz * full + (y_here - 1) * piece
                side_ref[0, base : base + piece, :] = block
            if dy == 2:
                side_ref[1, dz * full : dz * full + piece, :] = block

    def deep(tap, carry):
        base = pl.multiple_of(tap * WINDOW, WINDOW)
        for h in range(2):
            w2_ref[h, pl.ds(base, WINDOW), :] = spread_tap(
                k2_ref, tap, r2_ref[h], c2_ref[h], m2_ref.at[h]
            )
            w3_ref[h, pl.ds(base, WINDOW), :] = spread_tap(
                k3_ref, tap, r3_ref[h], c3_ref[h], m3_ref.at[h]
            )
        return carry

    lax.fori_loop(0, 9, deep, 0)


def expand_weights(first, second, third, y_here, xs):
    channels, parts = first.shape[:2]
    full = round_up(y_here * parts * xs, 128)
    lanes = xs * channels
    by_tap = [
        jnp.transpose(w, (2, 4, 3, 1, 0)).reshape(9, 3, w.shape[1], channels)
        for w in (first, second, third)
    ]
    maps = first_maps(parts, xs, channels)
    maps += spread_maps(xs, channels, True) + spread_maps(xs, channels, False)
    return pl.pallas_call(
        functools.partial(expand_kernel, y_here),
        out_shape=(
            jax.ShapeDtypeStruct((y_here, 3 * full, lanes), BF16),
            jax.ShapeDtypeStruct((2, 3 * full, lanes), BF16),
            jax.ShapeDtypeStruct((2, 9 * WINDOW, WINDOW), BF16),
            jax.ShapeDtypeStruct((2, 9 * WINDOW, xs // 2 * channels), BF16),
        ),
        in_specs=[vmem_spec()] * 12,
        out_specs=(vmem_spec(),) * 4,
        compiler_params=params(),
        cost_estimate=pl.CostEstimate(
            flops=20_000_000_000, bytes_accessed=10_000_000, transcendentals=0
        ),
    )(*by_tap, *maps)


def join(left, right):
    return jnp.concatenate(
        [left[:, :128], left[:, 128:] + right[:, :128], right[:, 128:]], axis=1
    )


def down_one(block):
    rolled = pltpu.roll(block, 1, 0)
    row = lax.broadcasted_iota(jnp.int32, block.shape, 0)
    return jnp.where(row == 0, 0.0, rolled)


def up_one(block):
    count = block.shape[0]
    rolled = pltpu.roll(block, count - 1, 0)
    row = lax.broadcasted_iota(jnp.int32, block.shape, 0)
    return jnp.where(row == count - 1, 0.0, rolled)


def net_kernel(
    place_ref,
    in_ref,
    w1_far,
    w1_side_far,
    w2_far,
    w3_far,
    b12_ref,
    b3_ref,
    order_ref,
    out_ref,
    spread,
    own,
    before,
    after,
    act1,
    act2,
    w1_ref,
    w1_side_ref,
    w2_ref,
    w3_ref,
    sems,
):
    devices, rows_in, lanes_in = in_ref.shape
    z1, groups = act1.shape[:2]
    z2 = act2.shape[0]
    z_here = z2 - 2
    y_here = groups - 2
    first_z = place_ref[0]
    z_count = place_ref[1]
    window = 256
    lanes = act1.shape[3]

    def taps(act, z, count, h):
        start = h * (lanes - window)
        pieces = []
        for dz in range(3):
            for dy in range(3):
                piece = act[pl.ds(z + dz, count), dy : dy + y_here, :, start : start + window]
                pieces.append(piece.reshape(count * y_here * devices, window))
        return jnp.concatenate(pieces, axis=1)

    first_copies = [
        pltpu.make_async_copy(w1_far.at[m], w1_ref.at[m], sems.at[m]) for m in range(y_here)
    ]
    side_copy = pltpu.make_async_copy(w1_side_far, w1_side_ref, sems.at[y_here])
    second_copy = pltpu.make_async_copy(w2_far, w2_ref, sems.at[y_here + 1])
    third_copy = pltpu.make_async_copy(w3_far, w3_ref, sems.at[y_here + 2])

    @pl.when(pl.program_id(0) == 0)
    def _():
        side_copy.start()
        for copy in first_copies:
            copy.start()
        second_copy.start()
        third_copy.start()
        for s in range(devices):
            piece = in_ref[s].astype(F32)
            for j in range(0, lanes_in, 128):
                spread[j // 128, pl.ds(s, rows_in, stride=devices), :] = piece[:, j : j + 128]

        tiles = [spread.at[j] for j in range(lanes_in // 128)]

        def shift(z, carry):
            base = pl.multiple_of(z * devices, devices)
            block = jnp.concatenate([part[pl.ds(base, devices), :] for part in tiles], axis=1)
            own[pl.ds(base, devices), :] = block.astype(BF16)
            before[pl.ds(base, devices), :] = down_one(block).astype(BF16)
            after[pl.ds(base, devices), :] = up_one(block).astype(BF16)
            return carry

        lax.fori_loop(0, z1 + 2, shift, 0)

        def three(ref):
            count = z1 * devices
            return jnp.concatenate(
                [ref[dz * devices : dz * devices + count, :] for dz in range(3)], axis=1
            )

        side_copy.wait()
        for m in range(y_here):
            first_copies[m].wait()
            result = jnp.dot(three(own), w1_ref[m], preferred_element_type=F32)
            if m == 0:
                result += jnp.dot(three(before), w1_side_ref[0], preferred_element_type=F32)
            if m == y_here - 1:
                result += jnp.dot(three(after), w1_side_ref[1], preferred_element_type=F32)
            value = jnp.maximum(result + b12_ref[0:1, :], 0.0).reshape(z1, devices, lanes)
            act1[:, m + 1] = value.astype(BF16)
            for z in range(z1):
                if m == 0:
                    act1[z, groups - 1] = up_one(value[z]).astype(BF16)
                if m == y_here - 1:
                    act1[z, 0] = down_one(value[z]).astype(BF16)
        for z in (0, 1, z1 - 2, z1 - 1):
            here = first_z + z - 2

            @pl.when((here < 0) | (here >= z_count))
            def _():
                act1[z] = jnp.zeros_like(act1[z])

        many = min(SECOND_GROUP, z2)

        def second(step, carry):
            z = step * many
            left = jnp.dot(taps(act1, z, many, 0), w2_ref[0], preferred_element_type=F32)
            right = jnp.dot(taps(act1, z, many, 1), w2_ref[1], preferred_element_type=F32)
            value = jnp.maximum(join(left, right) + b12_ref[1:2, :], 0.0)
            cube = value.reshape(many, y_here, devices, lanes)
            act2[pl.ds(z, many), 1 : groups - 1] = cube.astype(BF16)
            for i in range(many):
                act2[z + i, groups - 1] = up_one(cube[i, 0]).astype(BF16)
                act2[z + i, 0] = down_one(cube[i, y_here - 1]).astype(BF16)
            return carry

        second_copy.wait()
        lax.fori_loop(0, z2 // many, second, 0)
        third_copy.wait()
        for z in (0, z2 - 1):
            here = first_z + z - 1

            @pl.when((here < 0) | (here >= z_count))
            def _():
                act2[z] = jnp.zeros_like(act2[z])

    channels, many, xs, y_count = out_ref.shape
    z = pl.program_id(0) * many
    parts = []
    for h in range(2):
        result = jnp.dot(taps(act2, z, many, h), w3_ref[h], preferred_element_type=F32)
        value = jnp.maximum(result + b3_ref[...], 0.0).astype(BF16)
        parts.append(value)
    for i in range(many):
        pieces = []
        for value in parts:
            turned = lax.dot_general(
                value[i * y_count : (i + 1) * y_count],
                order_ref[...],
                (((0,), (0,)), ((), ())),
                preferred_element_type=F32,
            )
            pieces.append(turned.reshape(channels, xs // 2, y_count))
        out_ref[:, i] = jnp.concatenate(pieces, axis=1).astype(BF16)


def network(gathered, place, weights, biases, z_here, xs, y_here):
    devices, rows_in, lanes_in = gathered.shape
    channels = biases[0].shape[0]
    y_count = y_here * devices
    lanes = xs * channels
    w1, w1_side, w2, w3 = weights
    b12 = jnp.stack([jnp.tile(biases[0], xs), jnp.tile(biases[1], xs)])
    b3 = jnp.repeat(biases[2], xs // 2)[None]
    row = np.arange(y_count)
    order = np.zeros((y_count, y_count), np.float32)
    order[row, row % devices * y_here + row // devices] = 1.0
    order = jnp.asarray(order, BF16)
    z1, z2 = z_here + 4, z_here + 2
    step = min(THIRD_GROUP, z_here)
    groups = y_here + 2
    return pl.pallas_call(
        net_kernel,
        out_shape=jax.ShapeDtypeStruct((channels, z_here, xs, y_count), BF16),
        grid=(z_here // step,),
        in_specs=[pl.BlockSpec(memory_space=pltpu.SMEM), vmem_spec()]
        + [pl.BlockSpec(memory_space=pl.ANY)] * 4
        + [vmem_spec()] * 3,
        out_specs=pl.BlockSpec((channels, step, xs, y_count), lambda z: (0, z, 0, 0)),
        scratch_shapes=[
            pltpu.VMEM((lanes_in // 128, rows_in * devices, 128), F32),
            pltpu.VMEM((rows_in * devices, lanes_in), BF16),
            pltpu.VMEM((rows_in * devices, lanes_in), BF16),
            pltpu.VMEM((rows_in * devices, lanes_in), BF16),
            pltpu.VMEM((z1, groups, devices, lanes), BF16),
            pltpu.VMEM((z2, groups, devices, lanes), BF16),
            pltpu.VMEM(w1.shape, BF16),
            pltpu.VMEM(w1_side.shape, BF16),
            pltpu.VMEM(w2.shape, BF16),
            pltpu.VMEM(w3.shape, BF16),
            pltpu.SemaphoreType.DMA((y_here + 3,)),
        ],
        compiler_params=params(),
    )(place, gathered, w1, w1_side, w2, w3, b12, b3, order)


def on_device(
    kspace,
    sensitivity,
    weight_first,
    bias_first,
    weight_second,
    bias_second,
    weight_third,
    bias_third,
):
    devices = lax.axis_size("kz")
    _, y_here, _, xs, z_count = sensitivity.shape
    z_here = z_count // devices
    lines = y_transform(kspace, devices)
    received = lax.all_to_all(lines, "kz", 0, 0)
    weights = expand_weights(weight_first, weight_second, weight_third, y_here, xs)
    received, weights = lax.optimization_barrier((received, weights))
    merged = z_transform(received, sensitivity, devices)
    gathered = lax.all_to_all(merged, "kz", 0, 0)
    place = jnp.stack([lax.axis_index("kz") * z_here, z_count]).astype(jnp.int32)
    biases = (bias_first, bias_second, bias_third)
    return network(gathered, place, weights, biases, z_here, xs, y_here)


def solution(mesh):
    in_specs = (
        P("grp", None, "kz", None),
        P(None, ("grp", "kz"), None, None, None),
        P(),
        P(),
        P(),
        P(),
        P(),
        P(),
    )
    out_specs = P("grp", "kz", None, None)
    return jax.shard_map(
        on_device, mesh=mesh, in_specs=in_specs, out_specs=out_specs, check_vma=False
    )
```
